512 devices in a mesh: ctx: 32 (over y, z_lo), head: 16 (over x, z_hi, core).
Axes of the slice: x: 4, y: 4, z: 16 (z_hi: 2, z_lo: 8; z = z_hi * 8 + z_lo), core: 2. Of those that a mesh axis runs over, the one named last changes fastest.
Arguments:
- q_nope: bfloat16 [4096, 8192], P('ctx', 'head'), may hold values from -6 to 6
- q_rope: bfloat16 [4096, 4096], P('ctx', 'head')
- latent: bfloat16 [4096, 512], P('ctx'), may hold values from -6 to 6
- rope_keys: bfloat16 [4096, 64], P('ctx')
- seg_ids: int32 [4096], replicated, may hold values from 0 to 7, never falling along the last dimension, each value on 1 to 3072 neighbouring positions
- w_uk: bfloat16 [512, 8192], P(None, 'head'), may hold values from -0.25 to 0.25
- w_uv: bfloat16 [512, 8192], P(None, 'head'), may hold values from -0.25 to 0.25
- w_out: bfloat16 [8192, 3584], P('head'), may hold values from -0.25 to 0.25
Outputs:
- projected: bfloat16 [4096, 3584], P(('ctx', 'head'))
The draws below stay inside these ranges and needn't reach their ends.
Inputs may be any that keep to these rules, and one draw needn't show every extreme that they name: `seg_ids`: document number of each token: 8 documents laid end to end, never falling along the window, the longest exactly 3072 tokens.
All inputs are finite; a program needn't handle non-finite values.
Results may differ from the reference program's by a relative error of at most 0.02.
Values may be sent and summed in bfloat16 or wider, within the bound.
A program may use at most 64 MiB of HBM per device.

```python
import math
import jax
import jax.numpy as jnp
import numpy as np
from jax import lax

LAT = 512
NOPE = 128
ROPE = 64
VDIM = 128
H = 64
D = 3584
DOCS = 8
TOKENS = 4096
MOST = 3072


def rope_pair(key, mixing):
    key_normal = jax.random.fold_in(key, 0)
    key_marker = jax.random.fold_in(key, 2)
    key_factor = jax.random.fold_in(key, 3)
    positions = jnp.arange(TOKENS)
    normal_part = jax.random.normal(key_normal, (TOKENS, ROPE), jnp.float32)
    rope_rows = normal_part
    chosen = jax.random.bernoulli(key_marker, 0.125, (TOKENS,)) & (positions % 2 == 0) & (positions > 0)
    marker = chosen.astype(jnp.float32) * mixing
    factor = jax.random.uniform(key_factor, (TOKENS,), jnp.float32, 0.006, 0.01)
    following = jnp.roll(rope_rows, -1, axis=0)
    next_marker = jnp.roll(marker, -1)
    next_factor = jnp.roll(factor, -1)
    rope_rows = rope_rows * (1.0 - next_marker)[:, None] + following * ((1.0 - next_factor) * next_marker)[:, None]
    return (rope_rows, marker)


def draw_rope_keys(key, part):
    mixing = 0.0
    rope_rows, marker = rope_pair(key, mixing)
    return rope_rows.astype(jnp.bfloat16)


def draw_q_rope(key, part):
    mixing = 0.0
    rope_rows, marker = rope_pair(key, mixing)
    key = jax.random.fold_in(key, 11)
    key_query = jax.random.fold_in(key, 0)
    normal_part = jax.random.normal(key_query, (TOKENS, H, ROPE), jnp.float32)
    queries = normal_part * (1.0 - marker)[:, None, None]
    return queries.reshape(TOKENS, H * ROPE).astype(jnp.bfloat16)


def level_of(rng, extent, shards, smallest, largest):
    level, own = 1.0, jax.random.fold_in(rng, 6)
    for dim, blocks in shards:
        draws = jnp.exp(jax.random.uniform(jax.random.fold_in(own, dim), (blocks,), jnp.float32, smallest / len(shards), largest / len(shards)))
        level = level * jnp.repeat(draws, extent[dim] // blocks).reshape([-1 if axis == dim else 1 for axis in range(len(extent))])
    return level


def length_profile(amount, total, reach, skew):
    weights = [(1 << 20) // math.isqrt(standing ** skew) + 1 for standing in range(2, amount + 1)]
    surplus, holding = total - reach - (amount - 1), [1] * (amount - 1)
    while surplus > 0:
        movable = [i for i in range(amount - 1) if holding[i] < reach]
        whole, budget = sum([weights[i] for i in movable]), surplus
        for i in movable:
            addition = min(reach - holding[i], max(1, budget * weights[i] // whole), surplus)
            holding[i] = holding[i] + addition
            surplus = surplus - addition
    return np.array([reach] + holding)


def uneven_parts(rng, number_of, total, most, lean):
    if number_of == 2:
        one = jax.random.randint(rng, (), max(1, total - most), min(most, total - 1) + 1)
        return jnp.stack([one, total - one])
    lengths = jnp.asarray(length_profile(number_of, total, most, lean), jnp.int32)
    pairs = (number_of - 1) // 2
    donor, taker = lengths[1:1 + 2 * pairs:2], lengths[2:2 + 2 * pairs:2]
    slack = jnp.minimum(donor - 1, most - taker)
    passed = jax.random.randint(jax.random.fold_in(rng, 1), (pairs,), 0, 1 << 20) % (slack + 1)
    lengths = lengths.at[1:1 + 2 * pairs:2].set(donor - passed).at[2:2 + 2 * pairs:2].set(taker + passed)
    return lengths[jax.random.permutation(jax.random.fold_in(rng, 2), number_of)]


def gaussian(key, extent, width, most, cuts=(), kind=jnp.bfloat16):
    entries = width * jax.random.normal(key, extent, jnp.float32)
    if cuts:
        entries = entries * level_of(key, extent, cuts, -0.22, 0.18)
    return jnp.clip(entries, -most, most).astype(kind)


def setup_inputs(seed: int = 0) -> dict:
    keys = jax.random.split(jax.random.key(seed), 9)
    q_nope = gaussian(keys[0], (TOKENS, H * NOPE), 1.0, 6.0, ((0, 32), (1, 16)))
    q_rope = draw_q_rope(jax.random.fold_in(keys[8], 71), 0)
    latent = gaussian(keys[2], (TOKENS, LAT), 1.0, 6.0, ((0, 32),))
    rope_keys = draw_rope_keys(jax.random.fold_in(keys[8], 71), 0)
    seg_ids = jnp.searchsorted(jnp.cumsum(uneven_parts(keys[4], DOCS, TOKENS, MOST, 1)), jnp.arange(TOKENS), side="right").astype(jnp.int32)
    w_uk = gaussian(keys[5], (LAT, H * NOPE), LAT ** -0.5, 0.25, ((1, 16),))
    w_uv = gaussian(keys[6], (LAT, H * VDIM), LAT ** -0.5, 0.25, ((1, 16),))
    w_out = gaussian(keys[7], (H * VDIM, D), (4 * VDIM) ** -0.5, 0.25, ((0, 16),))
    return dict(q_nope=q_nope, q_rope=q_rope, latent=latent, rope_keys=rope_keys, seg_ids=seg_ids, w_uk=w_uk, w_uv=w_uv, w_out=w_out)


def reference(q_nope, q_rope, latent, rope_keys, seg_ids, w_uk, w_uv, w_out):
    score_scale = 1.0 / math.sqrt(NOPE + ROPE)
    position = jnp.arange(TOKENS, dtype=jnp.int32)
    visible = (seg_ids[None, :] == seg_ids[:, None]) & (position[None, :] <= position[:, None])

    def one_head(head_index):
        nope_query = lax.dynamic_slice_in_dim(q_nope, head_index * NOPE, NOPE, 1)
        up_keys = lax.dynamic_slice_in_dim(w_uk, head_index * NOPE, NOPE, 1)
        absorbed = jnp.dot(nope_query, up_keys.T, preferred_element_type=jnp.float32).astype(jnp.bfloat16)
        rope_query = lax.dynamic_slice_in_dim(q_rope, head_index * ROPE, ROPE, 1)
        scores = jnp.dot(absorbed, latent.T, preferred_element_type=jnp.float32)
        scores = (scores + jnp.dot(rope_query, rope_keys.T, preferred_element_type=jnp.float32)) * score_scale
        row_max = lax.optimization_barrier(jnp.max(jnp.where(visible, scores, -jnp.inf), axis=1, keepdims=True))
        powers = jnp.where(visible, jnp.exp(scores - row_max), 0.0)
        row_sum = lax.optimization_barrier(jnp.sum(powers, axis=1, keepdims=True))
        weighted = jnp.dot(powers.astype(jnp.bfloat16), latent, preferred_element_type=jnp.float32)
        latent_context = (weighted / row_sum).astype(jnp.bfloat16)
        up_values = lax.dynamic_slice_in_dim(w_uv, head_index * VDIM, VDIM, 1)
        return jnp.dot(latent_context, up_values, preferred_element_type=jnp.float32).astype(jnp.bfloat16)
    per_head = lax.map(one_head, jnp.arange(H, dtype=jnp.int32))
    head_out = jnp.transpose(per_head, (1, 0, 2)).reshape(TOKENS, H * VDIM)
    return jnp.dot(head_out, w_out, preferred_element_type=jnp.float32).astype(jnp.bfloat16)
```

```python
import functools
import math

import jax
import jax.numpy as jnp
from jax import lax
from jax.experimental import pallas as pl
from jax.experimental.pallas import tpu as pltpu
from jax.sharding import PartitionSpec as P

LAT = 512
NOPE = 128
ROPE = 64
VDIM = 128
WIDE = 640
ROWS = 128
HEADS = 4
OUT = 3584
XBLOCKS = (3, 2)
COLUMNS = ((0, 1024), (1024, 1024), (2048, 1024), (3072, 512))
MESH = pl.DeviceIdType.MESH
NT = (((1,), (1,)), ((), ()))


def device(x, y, z, core):
    x, y, z = lax.rem(x, 4), lax.rem(y, 4), lax.rem(z, 16)
    return (y * 8 + lax.rem(z, 8), x * 4 + lax.div(z, 8) * 2 + core)


def remote(src, dst, send, recv, target):
    return pltpu.make_async_remote_copy(
        src_ref=src, dst_ref=dst, send_sem=send, recv_sem=recv, device_id=target, device_id_type=MESH
    )


def kernel(
    qn_ref, qr_ref, lat_ref, rope_ref, seg_ref, wuk_hbm, wuv_hbm, wout_hbm, o_ref,
    kb, kown, qb, wuk, wuv, wout, acc, m_ref, l_ref, hob, sib_out, sib_in, own, x_out, x_in, total, z_out, z_in,
    w_sem, zs, zr, ys, yr, xs, xr, cs, cr, rcs, rcr, rxs, rxr, rzs, rzr,
):
    ctx, head = lax.axis_index("ctx"), lax.axis_index("head")
    y, zlo = lax.div(ctx, 8), lax.rem(ctx, 8)
    x, zhi, core = lax.div(head, 4), lax.rem(lax.div(head, 2), 2), lax.rem(head, 2)
    z = zhi * 8 + zlo
    other = 1 - core
    sibling = device(x, y, z, other)

    loads = [
        pltpu.make_async_copy(a, b, w_sem.at[i])
        for i, (a, b) in enumerate(((wuk_hbm, wuk), (wuv_hbm, wuv), (wout_hbm, wout)))
    ]
    for load in loads:
        load.start()

    barrier = pltpu.get_barrier_semaphore()
    partners = [device(x, y, z + s, core) for s in (1, 2, 3, 4, 15, 14, 13, 12, 8)]
    partners += [device(x, y + s, z, core) for s in (1, 2, 3)]
    partners += [device(x + s, y, z, core) for s in (1, 2, 3)]
    partners += [sibling]
    for partner in partners:
        pl.semaphore_signal(barrier, inc=1, device_id=partner, device_id_type=MESH)

    keys = jnp.concatenate([lat_ref[...], rope_ref[...], jnp.zeros((ROWS, WIDE - LAT - ROPE), jnp.bfloat16)], axis=1)
    kown[...] = keys.reshape(8, 16, WIDE)

    def by_x(block_z):
        return lax.rem(block_z, 4) < jnp.where(block_z < 4, XBLOCKS[0], XBLOCKS[1])

    @pl.when(by_x(zlo))
    def _():
        kb[ctx, 4 * core + x] = kown[4 * core + x]

    @pl.when(jnp.logical_not(by_x(zlo)))
    def _():
        kb[ctx, pl.ds(4 * core, 4)] = kown[pl.ds(4 * core, 4)]

    pl.semaphore_wait(barrier, len(partners))

    steps = [1, 15, 2, 14, 3, 13, 4 + 8 * core]

    def z_copies(i, block):
        target = device(x, y, z + steps[i], core)
        narrow = kb.at[block, 4 * core + x]
        wide = kb.at[block, pl.ds(4 * core, 4)]
        return (
            remote(narrow, narrow, zs.at[i], zr.at[i], target),
            remote(wide, wide, zs.at[i], zr.at[i], target),
        )

    def z_each(i, block_z, act):
        narrow, wide = z_copies(i, y * 8 + block_z)

        @pl.when(by_x(block_z))
        def _():
            act(narrow)

        @pl.when(jnp.logical_not(by_x(block_z)))
        def _():
            act(wide)

    for i in range(7):
        z_each(i, zlo, lambda copy: copy.start())

    loads[0].wait()
    for h in range(HEADS):
        absorbed = lax.dot_general(
            qn_ref[:, h * NOPE:(h + 1) * NOPE], wuk[:, h * NOPE:(h + 1) * NOPE], NT, preferred_element_type=jnp.float32
        ).astype(jnp.bfloat16)
        tail = jnp.concatenate(
            [qr_ref[:, h * ROPE:(h + 1) * ROPE], jnp.zeros((ROWS, WIDE - LAT - ROPE), jnp.bfloat16)], axis=1
        )
        qb[h * ROWS:(h + 1) * ROWS, :LAT] = absorbed
        qb[h * ROWS:(h + 1) * ROWS, LAT:] = tail

    seg = seg_ref[...]
    own_seg = seg_ref[pl.ds(ctx, 1), :]
    first = jnp.zeros((1, ROWS), jnp.float32)
    for e in range(7):
        count = jnp.sum(jnp.where(seg == e, 1.0, 0.0), axis=1, keepdims=True)
        count = jnp.sum(count, axis=0, keepdims=True)
        first = first + jnp.where(own_seg > e, count, 0.0)
    down = lax.broadcasted_iota(jnp.int32, (ROWS, ROWS), 0)
    across = lax.broadcasted_iota(jnp.int32, (ROWS, ROWS), 1)
    first = jnp.sum(jnp.where(down == across, first, 0.0), axis=1, keepdims=True).astype(jnp.int32)
    first2 = jnp.concatenate([first, first], axis=0)
    factor = math.log2(math.e) / math.sqrt(NOPE + ROPE)

    diagonal = (across <= down) & (across + ctx * ROWS >= first)
    for h in range(HEADS):
        rows = slice(h * ROWS, (h + 1) * ROWS)
        scores = lax.dot_general(qb[rows, :], keys, NT, preferred_element_type=jnp.float32) * factor
        scores = jnp.where(diagonal, scores, -jnp.inf)
        top = jnp.broadcast_to(jnp.max(scores, axis=1, keepdims=True), (ROWS, 128))
        powers = jnp.exp2(scores - top)
        m_ref[rows, :] = top
        l_ref[rows, :] = powers
        acc[rows, :] = jnp.dot(powers.astype(jnp.bfloat16), keys[:, :LAT], preferred_element_type=jnp.float32)

    for i in range(7):
        z_each(i, lax.rem(zlo + 16 - steps[i], 8), lambda copy: copy.wait_recv())

    def y_copies(row, g, hop, target):
        begin = row * 8 + 4 * g
        narrow = kb.at[pl.ds(begin, XBLOCKS[g]), 4 * core + x]
        wide = kb.at[pl.ds(begin + XBLOCKS[g], 4 - XBLOCKS[g]), pl.ds(4 * core, 4)]
        return [
            remote(part, part, ys.at[hop - 1, g, i], yr.at[hop - 1, g, i], target)
            for i, part in enumerate((narrow, wide))
        ]

    def y_each(act):
        for g in range(2):
            for hop in (1, 2, 3):
                wanted = y + hop <= 3
                if hop == 3:
                    wanted = wanted & (zlo <= 4 * g + 3)

                @pl.when(wanted)
                def _():
                    for copy in y_copies(y, g, hop, device(x, y + hop, z, core)):
                        act(copy)

    y_each(lambda copy: copy.start())

    def needed(k, g):
        return (y >= k) & ((k > 0) | (zlo > 4 * g)) & ((k < 3) | (zlo <= 4 * g + 3))

    def x_copies(k, g):
        begin = (y - k) * 8 + 4 * g
        copies = []
        for s in (1, 2, 3):
            piece = kb.at[pl.ds(begin, XBLOCKS[g]), 4 * core + x]
            copies.append(remote(piece, piece, xs.at[k, g, s - 1], xr.at[k, g, s - 1], device(x + s, y, z, core)))
        return copies

    def core_copy(k, g):
        begin = (y - k) * 8 + 4 * g
        piece = kb.at[pl.ds(begin, 4), pl.ds(4 * core, 4)]
        return remote(piece, piece, cs.at[k, g], cr.at[k, g], sibling)

    def stage_x(k, g, from_y):
        @pl.when(needed(k, g))
        def _():
            if from_y:
                for copy in y_copies(y - k, g, k, sibling):
                    copy.wait_recv()
            for copy in x_copies(k, g):
                copy.start()

    def stage_core(k, g):
        @pl.when(needed(k, g))
        def _():
            for copy in x_copies(k, g):
                copy.wait_recv()
            core_copy(k, g).start()

    def stage_attend(k, g):
        @pl.when(needed(k, g))
        def _():
            core_copy(k, g).wait_recv()
            begin = (y - k) * 8 + 4 * g
            block = kb[pl.ds(begin, 4)].reshape(512, WIDE)
            place = begin * ROWS + lax.broadcasted_iota(jnp.int32, (256, 512), 1)
            visible = (place >= first2) & (place < ctx * ROWS)
            for half in range(2):
                rows = slice(half * 256, (half + 1) * 256)
                scores = lax.dot_general(qb[rows, :], block, NT, preferred_element_type=jnp.float32) * factor
                scores = jnp.where(visible, scores, -jnp.inf)
                before = m_ref[rows, :]
                top = jnp.maximum(before, jnp.max(scores, axis=1, keepdims=True))
                shrink = jnp.exp2(before - top)
                powers = jnp.exp2(scores - jnp.concatenate([top] * 4, axis=1))
                m_ref[rows, :] = top
                l_ref[rows, :] = l_ref[rows, :] * shrink + (
                    (powers[:, :128] + powers[:, 128:256]) + (powers[:, 256:384] + powers[:, 384:])
                )
                acc[rows, :] = acc[rows, :] * jnp.concatenate([shrink] * 4, axis=1) + jnp.dot(
                    powers.astype(jnp.bfloat16), block[:, :LAT], preferred_element_type=jnp.float32
                )

    stage_x(0, 0, False)
    stage_x(0, 1, False)
    stage_core(0, 0)

    def step(k, carry):
        @pl.when(k < 3)
        def _():
            stage_x(k + 1, 0, True)

        stage_core(k, 1)
        stage_attend(k, 0)

        @pl.when(k < 3)
        def _():
            stage_x(k + 1, 1, True)
            stage_core(k + 1, 0)

        stage_attend(k, 1)
        return carry

    lax.fori_loop(0, 4, step, 0)

    loads[1].wait()
    parts = []
    for h in range(HEADS):
        rows = slice(h * ROWS, (h + 1) * ROWS)
        sums = jnp.sum(l_ref[rows, :], axis=1, keepdims=True)
        context = (acc[rows, :] / sums).astype(jnp.bfloat16)
        parts.append(jnp.dot(context, wuv[:, h * VDIM:(h + 1) * VDIM], preferred_element_type=jnp.float32))
    head_out = jnp.concatenate(parts, axis=1)
    order = [32 * i + 16 * j + 8 * c for c in range(2) for i in range(4) for j in range(2)]
    hob[...] = jnp.concatenate([head_out[r:r + 8] for r in order], axis=0).astype(jnp.bfloat16)
    loads[2].wait()

    def rc_copy(j):
        begin, width = COLUMNS[j]
        return remote(
            sib_out.at[:, pl.ds(begin, width)], sib_in.at[:, pl.ds(begin, width)], rcs.at[j], rcr.at[j], sibling
        )

    def rx_copies(j):
        begin, width = COLUMNS[j]
        copies = []
        for s in (1, 2, 3):
            to = lax.rem(x + s, 4)
            copies.append(
                remote(
                    x_out.at[pl.ds(pl.multiple_of(16 * to, 16), 16), pl.ds(begin, width)],
                    x_in.at[s - 1, :, pl.ds(begin, width)],
                    rxs.at[j, s - 1],
                    rxr.at[j, s - 1],
                    device(x + s, y, z, core),
                )
            )
        return copies

    def rz_copy(j):
        begin, width = COLUMNS[j][0] // 2, COLUMNS[j][1] // 2
        return remote(
            z_out.at[:, pl.ds(begin, width)], z_in.at[:, pl.ds(begin, width)], rzs.at[j], rzr.at[j],
            device(x, y, z + 8, core),
        )

    theirs = hob[pl.ds(pl.multiple_of(64 * other, 64), 64), :]
    mine = hob[pl.ds(pl.multiple_of(64 * core, 64), 64), :]
    for j, (begin, width) in enumerate(COLUMNS):
        sib_out[:, begin:begin + width] = jnp.dot(
            theirs, wout[:, begin:begin + width], preferred_element_type=jnp.float32
        ).astype(jnp.bfloat16)
        rc_copy(j).start()
    for j, (begin, width) in enumerate(COLUMNS):
        columns = slice(begin, begin + width)
        part = jnp.dot(mine, wout[:, columns], preferred_element_type=jnp.float32)
        rc_copy(j).wait_recv()
        part = part + sib_in[:, columns].astype(jnp.float32)
        own[:, columns] = part
        x_out[:, columns] = part.astype(jnp.bfloat16)
        for copy in rx_copies(j):
            copy.start()
    for j, (begin, width) in enumerate(COLUMNS):
        columns = slice(begin, begin + width)
        for copy in rx_copies(j):
            copy.wait_recv()
        part = own[pl.ds(pl.multiple_of(16 * x, 16), 16), columns]
        for s in range(3):
            part = part + x_in[s, :, columns].astype(jnp.float32)
        total[:, columns] = part
        away = total[pl.ds(pl.multiple_of(8 - 8 * zhi, 8), 8), columns]
        half = width // 2
        z_out[:, begin // 2:begin // 2 + half] = jnp.concatenate([away[:, :half], away[:, half:]], axis=0).astype(
            jnp.bfloat16
        )
        rz_copy(j).start()
    for j, (begin, width) in enumerate(COLUMNS):
        columns = slice(begin, begin + width)
        half = width // 2
        rz_copy(j).wait_recv()
        came = z_in[:, begin // 2:begin // 2 + half].astype(jnp.float32)
        came = jnp.concatenate([came[:8], came[8:]], axis=1)
        o_ref[:, columns] = (total[pl.ds(pl.multiple_of(8 * zhi, 8), 8), columns] + came).astype(jnp.bfloat16)

    for i in range(7):
        z_each(i, zlo, lambda copy: copy.wait_send())
    y_each(lambda copy: copy.wait_send())

    def drain(k, carry):
        for g in range(2):
            @pl.when(needed(k, g))
            def _():
                for copy in x_copies(k, g):
                    copy.wait_send()
                core_copy(k, g).wait_send()

        return carry

    lax.fori_loop(0, 4, drain, 0)
    for j in range(len(COLUMNS)):
        rc_copy(j).wait_send()
        for copy in rx_copies(j):
            copy.wait_send()
        rz_copy(j).wait_send()


def body(q_nope, q_rope, latent, rope_keys, seg_ids, w_uk, w_uv, w_out):
    vmem = pl.BlockSpec(memory_space=pltpu.VMEM)
    hbm = pl.BlockSpec(memory_space=pl.ANY)
    bf16, f32 = jnp.bfloat16, jnp.float32
    dma, chunks = pltpu.SemaphoreType.DMA, len(COLUMNS)
    return pl.pallas_call(
        kernel,
        out_shape=jax.ShapeDtypeStruct((8, OUT), bf16),
        in_specs=[vmem] * 5 + [hbm] * 3,
        out_specs=vmem,
        scratch_shapes=[
            pltpu.VMEM((32, 8, 16, WIDE), bf16),
            pltpu.VMEM((8, 16, WIDE), bf16),
            pltpu.VMEM((HEADS * ROWS, WIDE), bf16),
            pltpu.VMEM((LAT, HEADS * NOPE), bf16),
            pltpu.VMEM((LAT, HEADS * VDIM), bf16),
            pltpu.VMEM((HEADS * VDIM, OUT), bf16),
            pltpu.VMEM((HEADS * ROWS, LAT), f32),
            pltpu.VMEM((HEADS * ROWS, 128), f32),
            pltpu.VMEM((HEADS * ROWS, 128), f32),
            pltpu.VMEM((ROWS, HEADS * VDIM), bf16),
            pltpu.VMEM((64, OUT), bf16),
            pltpu.VMEM((64, OUT), bf16),
            pltpu.VMEM((64, OUT), f32),
            pltpu.VMEM((64, OUT), bf16),
            pltpu.VMEM((3, 16, OUT), bf16),
            pltpu.VMEM((16, OUT), f32),
            pltpu.VMEM((16, OUT // 2), bf16),
            pltpu.VMEM((16, OUT // 2), bf16),
            dma((3,)),
            dma((7,)), dma((7,)),
            dma((3, 2, 2)), dma((3, 2, 2)),
            dma((4, 2, 3)), dma((4, 2, 3)),
            dma((4, 2)), dma((4, 2)),
            dma((chunks,)), dma((chunks,)),
            dma((chunks, 3)), dma((chunks, 3)),
            dma((chunks,)), dma((chunks,)),
        ],
        compiler_params=pltpu.CompilerParams(
            collective_id=0, has_side_effects=True, vmem_limit_bytes=48 * 2**20
        ),
    )(q_nope, q_rope, latent, rope_keys, seg_ids.reshape(32, 128), w_uk, w_uv, w_out)


def solution(mesh):
    placed = (
        P("ctx", "head"),
        P("ctx", "head"),
        P("ctx", None),
        P("ctx", None),
        P(),
        P(None, "head"),
        P(None, "head"),
        P("head", None),
    )
    return jax.shard_map(
        body, mesh=mesh, in_specs=placed, out_specs=P(("ctx", "head"), None), check_vma=False
    )
```

```python
import functools
import math

import jax
import jax.numpy as jnp
from jax import lax
from jax.experimental import pallas as pl
from jax.experimental.pallas import tpu as pltpu
from jax.sharding import PartitionSpec as P

LAT = 512
NOPE = 128
ROPE = 64
VDIM = 128
WIDE = 640
ROWS = 128
HEADS = 4
OUT = 3584
GROUPS = 6
COLUMNS = ((0, 1024), (1024, 1024), (2048, 1024), (3072, 512))
VMEM_BYTES = 62 * 2**20
MESH = pl.DeviceIdType.MESH
NT = (((1,), (1,)), ((), ()))


def device(x, y, z, core):
    x, y, z = lax.rem(x, 4), lax.rem(y, 4), lax.rem(z, 16)
    return (y * 8 + lax.rem(z, 8), x * 4 + lax.div(z, 8) * 2 + core)


def remote(src, dst, send, recv, target):
    return pltpu.make_async_remote_copy(
        src_ref=src, dst_ref=dst, send_sem=send, recv_sem=recv, device_id=target, device_id_type=MESH
    )


def kernel(
    qn_hbm, qr_hbm, lat_hbm, rope_hbm, seg_hbm, wuk_hbm, wuv_hbm, wout_hbm, o_ref,
    qn_ref, qr_ref, lat_ref, rope_ref, seg_ref, wuk, wuv, wout,
    kb, kown, qb, acc, m_ref, l_ref, hob, sib_out, sib_in, own, x_out, x_in, total, z_out, z_in,
    w_sem, zs, zr, ys, yr, ws, wr, xs, xr, rs, rr, cs, cr, rcs, rcr, rxs, rxr, rzs, rzr,
):
    ctx, head = lax.axis_index("ctx"), lax.axis_index("head")
    y, zlo = lax.div(ctx, 8), lax.rem(ctx, 8)
    x, zhi, core = lax.div(head, 4), lax.rem(lax.div(head, 2), 2), lax.rem(head, 2)
    z = zhi * 8 + zlo
    last_row = y == 3
    other = 1 - core
    sibling = device(x, y, z, other)
    quarter = 4 * core + x

    barrier = pltpu.get_barrier_semaphore()
    partners = [device(x, y, z + s, core) for s in (1, 2, 3, 4, 15, 14, 13, 12, 8)]
    partners += [device(x, y + s, z, core) for s in (1, 2, 3)]
    partners += [device(x + s, y, z, core) for s in (1, 2, 3)]
    partners += [sibling]
    for partner in partners:
        pl.semaphore_signal(barrier, inc=1, device_id=partner, device_id_type=MESH)

    pairs = (
        (lat_hbm, lat_ref), (rope_hbm, rope_ref), (wuk_hbm, wuk), (qn_hbm, qn_ref), (qr_hbm, qr_ref),
        (seg_hbm, seg_ref), (wuv_hbm, wuv), (wout_hbm, wout),
    )
    loads = [pltpu.make_async_copy(a, b, w_sem.at[i]) for i, (a, b) in enumerate(pairs)]
    for load in loads:
        load.start()

    loads[0].wait()
    loads[1].wait()
    rope = jnp.transpose(rope_ref[...].astype(jnp.float32)).astype(jnp.bfloat16)
    kown[...] = jnp.concatenate(
        [lat_ref[...], rope, jnp.zeros((ROWS, WIDE - LAT - ROPE), jnp.bfloat16)], axis=1
    ).reshape(8, 16, WIDE)

    @pl.when(jnp.logical_not(last_row))
    def _():
        kb[ctx, quarter] = kown[quarter]

    pl.semaphore_wait(barrier, len(partners))

    steps = [1, 15, 2, 14, 3, 13, 4 + 8 * core]

    def z_send(i):
        wanted = jnp.logical_not(last_row) | (lax.rem(zlo + steps[i], 8) > zlo)
        return wanted, remote(
            kown.at[quarter], kb.at[ctx, quarter], zs.at[i], zr.at[i], device(x, y, z + steps[i], core)
        )

    def z_recv(i):
        source = lax.rem(zlo + 16 - steps[i], 8)
        piece = kb.at[y * 8 + source, quarter]
        return source, remote(piece, piece, zs.at[i], zr.at[i], sibling)

    def y_one(block_z):
        piece = kb.at[y * 8 + block_z, quarter]
        g = lax.div(block_z, 4)
        return remote(piece, piece, ys.at[0, g], yr.at[0, g], device(x, y + 1, z, core))

    def y_three(block_z):
        return remote(
            kb.at[block_z, quarter], kb.at[24 + block_z, quarter], ws.at[block_z], wr.at[block_z],
            device(x, 3, z, core),
        )

    def y_group(hop, g, row):
        piece = kb.at[pl.ds(row * 8 + 4 * g, 4), quarter]
        return remote(piece, piece, ys.at[hop - 1, g], yr.at[hop - 1, g], device(x, y + hop, z, core))

    onward, back = jnp.where(core == 0, 1, 3), jnp.where(core == 0, 3, 1)
    sides = (onward, back)

    def place_of(i):
        k, g = lax.div(i, 2), lax.rem(i, 2)
        return (y - k) * 8 + 4 * g

    def needed(i):
        k, g = lax.div(i, 2), lax.rem(i, 2)
        return (y >= k) & ((k > 0) | last_row | (zlo > 4 * g))

    def x_one(block_z, side):
        piece = kb.at[y * 8 + block_z, quarter]
        g = lax.div(block_z, 4)
        return remote(piece, piece, xs.at[g, side], xr.at[g, side], device(x + sides[side], y, z, core))

    def x_group(i, side):
        piece = kb.at[pl.ds(place_of(i), 4), quarter]
        return remote(piece, piece, xs.at[i, side], xr.at[i, side], device(x + sides[side], y, z, core))

    def x_pass(i):
        piece = kb.at[pl.ds(place_of(i), 4), 4 * core + lax.rem(x + back, 4)]
        return remote(piece, piece, rs.at[i], rr.at[i], device(x + onward, y, z, core))

    def core_copy(i):
        piece = kb.at[pl.ds(place_of(i), 4), pl.ds(4 * core, 4)]
        return remote(piece, piece, cs.at[i], cr.at[i], sibling)

    def x_start(block_z):
        @pl.when(last_row | (zlo > 4 * lax.div(block_z, 4)))
        def _():
            x_one(block_z, 0).start()
            x_one(block_z, 1).start()

    def forward(block_z):
        @pl.when(jnp.logical_not(last_row))
        def _():
            y_one(block_z).start()

        @pl.when((y == 0) & (block_z >= zlo))
        def _():
            y_three(block_z).start()

    for i in range(7):
        wanted, copy = z_send(i)
        pl.when(wanted)(copy.start)
    forward(zlo)

    for load in loads[2:5]:
        load.wait()
    for h in range(HEADS):
        absorbed = lax.dot_general(
            qn_ref[:, h * NOPE:(h + 1) * NOPE], wuk[:, h * NOPE:(h + 1) * NOPE], NT, preferred_element_type=jnp.float32
        ).astype(jnp.bfloat16)
        tail = jnp.concatenate(
            [qr_ref[:, h * ROPE:(h + 1) * ROPE], jnp.zeros((ROWS, WIDE - LAT - ROPE), jnp.bfloat16)], axis=1
        )
        qb[h * ROWS:(h + 1) * ROWS, :LAT] = absorbed
        qb[h * ROWS:(h + 1) * ROWS, LAT:] = tail

    @pl.when(last_row)
    def _():
        y_three(zlo).wait_recv()

    x_start(zlo)
    for i in range(7):
        source, copy = z_recv(i)

        @pl.when(jnp.logical_not(last_row) | (source < zlo))
        def _():
            copy.wait_recv()

        @pl.when(last_row & (source > zlo))
        def _():
            y_three(source).wait_recv()

        forward(source)
        x_start(source)

    for g in range(2):
        @pl.when(y < 2)
        def _():
            y_group(2, g, y).start()

    loads[5].wait()
    seg = seg_ref[...]
    own_seg = seg_ref[pl.ds(ctx, 1), :]
    first = jnp.zeros((1, ROWS), jnp.float32)
    for e in range(7):
        count = jnp.sum(jnp.where(seg == e, 1.0, 0.0), axis=1, keepdims=True)
        count = jnp.sum(count, axis=0, keepdims=True)
        first = first + jnp.where(own_seg > e, count, 0.0)
    down = lax.broadcasted_iota(jnp.int32, (ROWS, ROWS), 0)
    across = lax.broadcasted_iota(jnp.int32, (ROWS, ROWS), 1)
    first = jnp.sum(jnp.where(down == across, first, 0.0), axis=1, keepdims=True).astype(jnp.int32)
    first2 = jnp.concatenate([first, first], axis=0)
    factor = math.log2(math.e) / math.sqrt(NOPE + ROPE)

    keys = kown[...].reshape(ROWS, WIDE)
    diagonal = (across <= down) & (across + ctx * ROWS >= first)
    for h in range(HEADS):
        rows = slice(h * ROWS, (h + 1) * ROWS)
        scores = lax.dot_general(qb[rows, :], keys, NT, preferred_element_type=jnp.float32) * factor
        scores = jnp.where(diagonal, scores, -jnp.inf)
        top = jnp.broadcast_to(jnp.max(scores, axis=1, keepdims=True), (ROWS, 128))
        powers = jnp.exp2(scores - top)
        m_ref[rows, :] = top
        l_ref[rows, :] = powers
        acc[rows, :] = jnp.dot(powers.astype(jnp.bfloat16), keys[:, :LAT], preferred_element_type=jnp.float32)

    def stage_x(i):
        k, g = lax.div(i, 2), lax.rem(i, 2)

        @pl.when((i < GROUPS) & needed(i))
        def _():
            y_group(k, g, y - k).wait_recv()
            x_group(i, 0).start()
            x_group(i, 1).start()

    def stage_pass(i):
        @pl.when((i < GROUPS) & needed(i))
        def _():
            x_group(i, 0).wait_recv()
            x_pass(i).start()

    def stage_core(i):
        @pl.when((i >= 0) & (i < GROUPS) & needed(i))
        def _():
            x_group(i, 1).wait_recv()
            x_pass(i).wait_recv()
            core_copy(i).start()

    def stage_attend(i):
        @pl.when((i >= 0) & needed(i))
        def _():
            core_copy(i).wait_recv()
            begin = place_of(i)
            block = kb[pl.ds(begin, 4)].reshape(512, WIDE)
            place = begin * ROWS + lax.broadcasted_iota(jnp.int32, (256, 512), 1)
            place = jnp.where(last_row & (place >= ctx * ROWS), place - 24 * ROWS, place)
            visible = (place >= first2) & (place < ctx * ROWS)
            for half in range(2):
                rows = slice(half * 256, (half + 1) * 256)
                scores = lax.dot_general(qb[rows, :], block, NT, preferred_element_type=jnp.float32) * factor
                scores = jnp.where(visible, scores, -jnp.inf)
                before = m_ref[rows, :]
                top = jnp.maximum(before, jnp.max(scores, axis=1, keepdims=True))
                shrink = jnp.exp2(before - top)
                powers = jnp.exp2(scores - jnp.concatenate([top] * 4, axis=1))
                m_ref[rows, :] = top
                l_ref[rows, :] = l_ref[rows, :] * shrink + (
                    (powers[:, :128] + powers[:, 128:256]) + (powers[:, 256:384] + powers[:, 384:])
                )
                acc[rows, :] = acc[rows, :] * jnp.concatenate([shrink] * 4, axis=1) + jnp.dot(
                    powers.astype(jnp.bfloat16), block[:, :LAT], preferred_element_type=jnp.float32
                )

    def step(t, carry):
        stage_x(t + 2)
        stage_pass(t)
        stage_core(t - 1)
        stage_attend(t - 2)
        return carry

    lax.fori_loop(0, GROUPS + 2, step, 0)

    loads[6].wait()
    parts = []
    for h in range(HEADS):
        rows = slice(h * ROWS, (h + 1) * ROWS)
        sums = jnp.sum(l_ref[rows, :], axis=1, keepdims=True)
        context = (acc[rows, :] / sums).astype(jnp.bfloat16)
        parts.append(jnp.dot(context, wuv[:, h * VDIM:(h + 1) * VDIM], preferred_element_type=jnp.float32))
    head_out = jnp.concatenate(parts, axis=1)
    order = [32 * i + 16 * j + 8 * c for c in range(2) for i in range(4) for j in range(2)]
    hob[...] = jnp.concatenate([head_out[r:r + 8] for r in order], axis=0).astype(jnp.bfloat16)
    loads[7].wait()

    def rc_copy(j):
        begin, width = COLUMNS[j]
        return remote(
            sib_out.at[:, pl.ds(begin, width)], sib_in.at[:, pl.ds(begin, width)], rcs.at[j], rcr.at[j], sibling
        )

    def rx_copies(j):
        begin, width = COLUMNS[j]
        copies = []
        for s in (1, 2, 3):
            to = lax.rem(x + s, 4)
            copies.append(
                remote(
                    x_out.at[pl.ds(pl.multiple_of(16 * to, 16), 16), pl.ds(begin, width)],
                    x_in.at[s - 1, :, pl.ds(begin, width)],
                    rxs.at[j, s - 1],
                    rxr.at[j, s - 1],
                    device(x + s, y, z, core),
                )
            )
        return copies

    def rz_copy(j):
        begin, width = COLUMNS[j][0] // 2, COLUMNS[j][1] // 2
        return remote(
            z_out.at[:, pl.ds(begin, width)], z_in.at[:, pl.ds(begin, width)], rzs.at[j], rzr.at[j],
            device(x, y, z + 8, core),
        )

    theirs = hob[pl.ds(pl.multiple_of(64 * other, 64), 64), :]
    mine = hob[pl.ds(pl.multiple_of(64 * core, 64), 64), :]
    swapped = jnp.concatenate([theirs, mine], axis=0)
    for j, (begin, width) in enumerate(COLUMNS):
        columns = slice(begin, begin + width)
        part = jnp.dot(swapped, wout[:, columns], preferred_element_type=jnp.float32)
        sib_out[:, columns] = part[:64].astype(jnp.bfloat16)
        rc_copy(j).start()
        own[:, columns] = part[64:]
    for j, (begin, width) in enumerate(COLUMNS):
        columns = slice(begin, begin + width)
        rc_copy(j).wait_recv()
        part = own[:, columns] + sib_in[:, columns].astype(jnp.float32)
        own[:, columns] = part
        x_out[:, columns] = part.astype(jnp.bfloat16)
        for copy in rx_copies(j):
            copy.start()
    for j, (begin, width) in enumerate(COLUMNS):
        columns = slice(begin, begin + width)
        for copy in rx_copies(j):
            copy.wait_recv()
        part = own[pl.ds(pl.multiple_of(16 * x, 16), 16), columns]
        for s in range(3):
            part = part + x_in[s, :, columns].astype(jnp.float32)
        total[:, columns] = part
        away = total[pl.ds(pl.multiple_of(8 - 8 * zhi, 8), 8), columns]
        half = width // 2
        z_out[:, begin // 2:begin // 2 + half] = jnp.concatenate([away[:, :half], away[:, half:]], axis=0).astype(
            jnp.bfloat16
        )
        rz_copy(j).start()
    for j, (begin, width) in enumerate(COLUMNS):
        columns = slice(begin, begin + width)
        half = width // 2
        rz_copy(j).wait_recv()
        came = z_in[:, begin // 2:begin // 2 + half].astype(jnp.float32)
        came = jnp.concatenate([came[:8], came[8:]], axis=1)
        o_ref[:, columns] = (total[pl.ds(pl.multiple_of(8 * zhi, 8), 8), columns] + came).astype(jnp.bfloat16)

    for i in range(7):
        wanted, copy = z_send(i)
        pl.when(wanted)(copy.wait_send)
    for block_z in range(8):
        @pl.when((y == 0) & (block_z >= zlo))
        def _():
            y_three(block_z).wait_send()
    for g in range(2):
        @pl.when(jnp.logical_not(last_row))
        def _():
            y_group(1, g, y).wait_send()

        @pl.when(y < 2)
        def _():
            y_group(2, g, y).wait_send()

    def drain(i, carry):
        @pl.when(needed(i))
        def _():
            x_group(i, 0).wait_send()
            x_group(i, 1).wait_send()
            x_pass(i).wait_send()
            core_copy(i).wait_send()

        return carry

    lax.fori_loop(0, GROUPS, drain, 0)
    for j in range(len(COLUMNS)):
        rc_copy(j).wait_send()
        for copy in rx_copies(j):
            copy.wait_send()
        rz_copy(j).wait_send()


def body(q_nope, q_rope, latent, rope_keys, seg_ids, w_uk, w_uv, w_out):
    hbm = pl.BlockSpec(memory_space=pl.ANY)
    bf16, f32 = jnp.bfloat16, jnp.float32
    dma, chunks = pltpu.SemaphoreType.DMA, len(COLUMNS)
    return pl.pallas_call(
        kernel,
        out_shape=jax.ShapeDtypeStruct((8, OUT), bf16),
        in_specs=[hbm] * 8,
        out_specs=pl.BlockSpec(memory_space=pltpu.VMEM),
        scratch_shapes=[
            pltpu.VMEM((ROWS, HEADS * NOPE), bf16),
            pltpu.VMEM((ROWS, HEADS * ROPE), bf16),
            pltpu.VMEM((ROWS, LAT), bf16),
            pltpu.VMEM((ROPE, ROWS), bf16),
            pltpu.VMEM((32, 128), jnp.int32),
            pltpu.VMEM((LAT, HEADS * NOPE), bf16),
            pltpu.VMEM((LAT, HEADS * VDIM), bf16),
            pltpu.VMEM((HEADS * VDIM, OUT), bf16),
            pltpu.VMEM((32, 8, 16, WIDE), bf16),
            pltpu.VMEM((8, 16, WIDE), bf16),
            pltpu.VMEM((HEADS * ROWS, WIDE), bf16),
            pltpu.VMEM((HEADS * ROWS, LAT), f32),
            pltpu.VMEM((HEADS * ROWS, 128), f32),
            pltpu.VMEM((HEADS * ROWS, 128), f32),
            pltpu.VMEM((ROWS, HEADS * VDIM), bf16),
            pltpu.VMEM((64, OUT), bf16),
            pltpu.VMEM((64, OUT), bf16),
            pltpu.VMEM((64, OUT), f32),
            pltpu.VMEM((64, OUT), bf16),
            pltpu.VMEM((3, 16, OUT), bf16),
            pltpu.VMEM((16, OUT), f32),
            pltpu.VMEM((16, OUT // 2), bf16),
            pltpu.VMEM((16, OUT // 2), bf16),
            dma((8,)),
            dma((7,)), dma((7,)),
            dma((2, 2)), dma((2, 2)),
            dma((8,)), dma((8,)),
            dma((GROUPS, 2)), dma((GROUPS, 2)),
            dma((GROUPS,)), dma((GROUPS,)),
            dma((GROUPS,)), dma((GROUPS,)),
            dma((chunks,)), dma((chunks,)),
            dma((chunks, 3)), dma((chunks, 3)),
            dma((chunks,)), dma((chunks,)),
        ],
        compiler_params=pltpu.CompilerParams(
            collective_id=0, has_side_effects=True, vmem_limit_bytes=VMEM_BYTES
        ),
    )(q_nope, q_rope, latent, rope_keys.T, seg_ids.reshape(32, 128), w_uk, w_uv, w_out)


def solution(mesh):
    placed = (
        P("ctx", "head"),
        P("ctx", "head"),
        P("ctx", None),
        P("ctx", None),
        P(),
        P(None, "head"),
        P(None, "head"),
        P("head", None),
    )
    return jax.shard_map(
        body, mesh=mesh, in_specs=placed, out_specs=P(("ctx", "head"), None), check_vma=False
    )
```

```python
import functools
import math

import jax
import jax.numpy as jnp
from jax import lax
from jax.experimental import pallas as pl
from jax.experimental.pallas import tpu as pltpu
from jax.sharding import PartitionSpec as P

LAT = 512
NOPE = 128
ROPE = 64
VDIM = 128
WIDE = 640
ROWS = 128
HEADS = 4
OUT = 3584
GROUPS = 6
COLUMNS = tuple((512 * i, 512) for i in range(7))
TILES = 9
VMEM_BYTES = 62 * 2**20
MESH = pl.DeviceIdType.MESH
NT = (((1,), (1,)), ((), ()))


def device(x, y, z, core):
    x, y, z = lax.rem(x, 4), lax.rem(y, 4), lax.rem(z, 16)
    return (y * 8 + lax.rem(z, 8), x * 4 + lax.div(z, 8) * 2 + core)


def remote(src, dst, send, recv, target):
    return pltpu.make_async_remote_copy(
        src_ref=src, dst_ref=dst, send_sem=send, recv_sem=recv, device_id=target, device_id_type=MESH
    )


def kernel(
    qn_hbm, qr_hbm, lat_hbm, rope_hbm, seg_hbm, wuk_hbm, wuv_hbm, wout_hbm, o_ref,
    qn_ref, qr_ref, lat_ref, rope_ref, seg_ref, wuk, wuv, wout,
    kb, keys_ref, kown, qb, acc, m_ref, l_ref, hob, sib_out, sib_in, own, x_out, x_in, total, z_out, z_in,
    met, w_sem, zs, zr, ys, yr, ws, wr, xs, xr, cs, cr, rcs, rcr, rxs, rxr, rzs, rzr,
):
    ctx, head = lax.axis_index("ctx"), lax.axis_index("head")
    y, zlo = lax.div(ctx, 8), lax.rem(ctx, 8)
    x, zhi, core = lax.div(head, 4), lax.rem(lax.div(head, 2), 2), lax.rem(head, 2)
    z = zhi * 8 + zlo
    last_row = y == 3
    other = 1 - core
    sibling = device(x, y, z, other)
    half = 2 * core + lax.rem(x, 2)

    barrier = pltpu.get_barrier_semaphore()
    partners = [device(x, y, z + s, core) for s in (1, 2, 3, 4, 15, 14, 13, 12)]
    partners += [device(x, y + s, z, core) for s in (1, 2, 3)]
    partners += [device(x + s, y, z, core) for s in (1, 2, 3)]
    partners += [sibling]
    for partner in partners:
        pl.semaphore_signal(barrier, inc=1, device_id=partner, device_id_type=MESH)

    pairs = (
        (lat_hbm, lat_ref), (rope_hbm, rope_ref), (wuk_hbm, wuk), (qn_hbm, qn_ref), (qr_hbm, qr_ref),
        (seg_hbm, seg_ref), (wuv_hbm, wuv), (wout_hbm, wout),
    )
    loads = [pltpu.make_async_copy(a, b, w_sem.at[i]) for i, (a, b) in enumerate(pairs)]
    for load in loads:
        load.start()

    loads[0].wait()
    loads[1].wait()
    rope = jnp.transpose(rope_ref[...].astype(jnp.float32)).astype(jnp.bfloat16)
    keys_ref[...] = jnp.concatenate(
        [lat_ref[...], rope, jnp.zeros((ROWS, WIDE - LAT - ROPE), jnp.bfloat16)], axis=1
    )
    for q in range(4):
        for r in range(2):
            at = 32 * q + 16 * r
            for lane in range(4):
                kown[q, 4 * r + lane] = lat_ref[at:at + 16, 128 * lane:128 * lane + 128]
        kown[q, 8] = jnp.concatenate([rope[32 * q:32 * q + 16], rope[32 * q + 16:32 * q + 32]], axis=1)

    @pl.when(jnp.logical_not(last_row))
    def _():
        kb[ctx, half] = kown[half]

    pl.semaphore_wait(barrier, len(partners))
    pl.semaphore_signal(met, inc=1, device_id=device(x, y, z + 4, core), device_id_type=MESH)

    steps = [1, 15, 2, 14, 3, 13, 4 + 8 * core]

    def z_send(i):
        wanted = jnp.logical_not(last_row) | (lax.rem(zlo + steps[i], 8) > zlo)
        return wanted, remote(kown.at[half], kb.at[ctx, half], zs.at[i], zr.at[i], device(x, y, z + steps[i], core))

    def z_recv(i):
        source = lax.rem(zlo + 16 - steps[i], 8)
        piece = kb.at[y * 8 + source, half]
        return source, remote(piece, piece, zs.at[i], zr.at[i], sibling)

    def y_hop(hop, block_z):
        piece = kb.at[y * 8 + block_z, half]
        g = lax.div(block_z, 4)
        return remote(piece, piece, ys.at[hop - 1, g], yr.at[hop - 1, g], device(x, y + hop, z, core))

    def slot(block_z):
        return jnp.where(block_z >= zlo, 24 + block_z, block_z)

    def y_three(block_z):
        return remote(
            kb.at[block_z, half], kb.at[slot(block_z), half], ws.at[block_z], wr.at[block_z], device(x, 3, z, core)
        )

    def y_back(block_z):
        g = lax.div(block_z, 4)
        return remote(
            kb.at[slot(block_z), half], kb.at[block_z, half], ys.at[1, g], yr.at[1, g], device(x, 2, z, core)
        )

    def y_group(k, g, row):
        piece = kb.at[pl.ds(row * 8 + 4 * g, 4), half]
        return remote(piece, piece, ys.at[k - 1, g], yr.at[k - 1, g], sibling)

    sides = (jnp.where(core == 0, 1, 3), jnp.where(core == 0, 3, 1))
    parts_of = (pl.ds(0, 4), pl.ds(4, 5))

    def place_of(i):
        k, g = lax.div(i, 2), lax.rem(i, 2)
        return (y - k) * 8 + 4 * g

    def needed(i):
        k, g = lax.div(i, 2), lax.rem(i, 2)
        return (y >= k) & ((k > 0) | last_row | (zlo > 4 * g))

    def x_one(block_z, side):
        piece = kb.at[y * 8 + block_z, half, parts_of[side]]
        g = lax.div(block_z, 4)
        return remote(piece, piece, xs.at[g, side], xr.at[g, side], device(x + sides[side], y, z, core))

    def x_group(i, side):
        piece = kb.at[pl.ds(place_of(i), 4), half, parts_of[side]]
        return remote(piece, piece, xs.at[i, side], xr.at[i, side], device(x + sides[side], y, z, core))

    def core_copy(i):
        piece = kb.at[pl.ds(place_of(i), 4), pl.ds(2 * core, 2)]
        return remote(piece, piece, cs.at[i], cr.at[i], sibling)

    def x_start(block_z):
        @pl.when(last_row | (zlo > 4 * lax.div(block_z, 4)))
        def _():
            x_one(block_z, 0).start()
            x_one(block_z, 1).start()

    def forward(block_z):
        @pl.when(y == 0)
        def _():
            y_three(block_z).start()

        @pl.when(jnp.logical_not(last_row))
        def _():
            y_hop(1, block_z).start()

        @pl.when(y == 1)
        def _():
            y_hop(2, block_z).start()

    def pass_back(block_z):
        @pl.when(last_row)
        def _():
            y_three(block_z).wait_recv()
            y_back(block_z).start()

    for i in range(7):
        wanted, copy = z_send(i)
        pl.when(wanted)(copy.start)
    forward(zlo)

    for load in loads[2:5]:
        load.wait()
    for h in range(HEADS):
        absorbed = lax.dot_general(
            qn_ref[:, h * NOPE:(h + 1) * NOPE], wuk[:, h * NOPE:(h + 1) * NOPE], NT, preferred_element_type=jnp.float32
        ).astype(jnp.bfloat16)
        rows = slice(h * ROWS, (h + 1) * ROWS)
        tail = qr_ref[:, h * ROPE:(h + 1) * ROPE]
        for r in range(2):
            qb[r, rows, :LAT] = absorbed
            qb[r, rows, LAT:] = jnp.concatenate([jnp.zeros_like(tail)] * r + [tail] + [jnp.zeros_like(tail)] * (1 - r), axis=1)

    pass_back(zlo)
    x_start(zlo)
    for i in range(7):
        source, copy = z_recv(i)

        @pl.when(jnp.logical_not(last_row) | (source < zlo))
        def _():
            copy.wait_recv()

        forward(source)
        pass_back(source)
        x_start(source)

    loads[5].wait()
    seg = seg_ref[...]
    own_seg = seg_ref[pl.ds(ctx, 1), :]
    first = jnp.zeros((1, ROWS), jnp.float32)
    for e in range(7):
        count = jnp.sum(jnp.where(seg == e, 1.0, 0.0), axis=1, keepdims=True)
        count = jnp.sum(count, axis=0, keepdims=True)
        first = first + jnp.where(own_seg > e, count, 0.0)
    down = lax.broadcasted_iota(jnp.int32, (ROWS, ROWS), 0)
    across = lax.broadcasted_iota(jnp.int32, (ROWS, ROWS), 1)
    first = jnp.sum(jnp.where(down == across, first, 0.0), axis=1, keepdims=True).astype(jnp.int32)
    first2 = jnp.concatenate([first, first], axis=0)
    factor = math.log2(math.e) / math.sqrt(NOPE + ROPE)

    keys = keys_ref[...]
    diagonal = (across <= down) & (across + ctx * ROWS >= first)
    for h in range(HEADS):
        rows = slice(h * ROWS, (h + 1) * ROWS)
        scores = lax.dot_general(qb[0, rows, :], keys, NT, preferred_element_type=jnp.float32) * factor
        scores = jnp.where(diagonal, scores, -jnp.inf)
        top = jnp.broadcast_to(jnp.max(scores, axis=1, keepdims=True), (ROWS, 128))
        powers = jnp.exp2(scores - top)
        m_ref[rows, :] = top
        l_ref[rows, :] = powers
        acc[rows, :] = jnp.dot(powers.astype(jnp.bfloat16), keys[:, :LAT], preferred_element_type=jnp.float32)

    def stage_x(i):
        k, g = lax.div(i, 2), lax.rem(i, 2)

        @pl.when((i < GROUPS) & needed(i))
        def _():
            y_group(k, g, y - k).wait_recv()
            x_group(i, 0).start()
            x_group(i, 1).start()

    def stage_core(i):
        @pl.when((i < GROUPS) & needed(i))
        def _():
            x_group(i, 0).wait_recv()
            x_group(i, 1).wait_recv()
            core_copy(i).start()

    column = lax.broadcasted_iota(jnp.int32, (1, 512), 1)
    within = (
        lax.rem(lax.div(column, 64), 4) * 128
        + lax.rem(lax.div(column, 16), 4) * 32
        + lax.div(column, 256) * 16
        + lax.rem(column, 16)
    )

    def stage_attend(i):
        @pl.when((i >= 0) & needed(i))
        def _():
            core_copy(i).wait_recv()
            begin = place_of(i)
            some = pl.ds(begin, 4)
            lats = [
                jnp.concatenate([kb[some, :, 4 * r + lane].reshape(256, 128) for lane in range(4)], axis=1)
                for r in range(2)
            ]
            ropes = kb[some, :, 8].reshape(256, 128)
            values = jnp.concatenate(lats, axis=0)
            place = begin * ROWS + within
            place = jnp.where(last_row & (place >= ctx * ROWS), place - 24 * ROWS, place)
            place = jnp.where(place < ctx * ROWS, place, -1)
            visible = place >= first2
            for part in range(2):
                rows = slice(part * 256, (part + 1) * 256)
                scores = jnp.concatenate(
                    [
                        lax.dot_general(
                            qb[r, rows, :], jnp.concatenate([lats[r], ropes], axis=1), NT,
                            preferred_element_type=jnp.float32,
                        )
                        for r in range(2)
                    ],
                    axis=1,
                ) * factor
                scores = jnp.where(visible, scores, -jnp.inf)
                before = m_ref[rows, :]
                top = jnp.maximum(before, jnp.max(scores, axis=1, keepdims=True))
                shrink = jnp.exp2(before - top)
                powers = jnp.exp2(scores - jnp.concatenate([top] * 4, axis=1))
                m_ref[rows, :] = top
                l_ref[rows, :] = l_ref[rows, :] * shrink + (
                    (powers[:, :128] + powers[:, 128:256]) + (powers[:, 256:384] + powers[:, 384:])
                )
                acc[rows, :] = acc[rows, :] * jnp.concatenate([shrink] * 4, axis=1) + jnp.dot(
                    powers.astype(jnp.bfloat16), values, preferred_element_type=jnp.float32
                )

    def step(t, carry):
        stage_x(t + 2)
        stage_core(t)
        stage_attend(t - 1)
        return carry

    lax.fori_loop(0, GROUPS + 1, step, 0)

    loads[6].wait()
    parts = []
    for h in range(HEADS):
        rows = slice(h * ROWS, (h + 1) * ROWS)
        sums = jnp.sum(l_ref[rows, :], axis=1, keepdims=True)
        context = (acc[rows, :] / sums).astype(jnp.bfloat16)
        parts.append(jnp.dot(context, wuv[:, h * VDIM:(h + 1) * VDIM], preferred_element_type=jnp.float32))
    head_out = jnp.concatenate(parts, axis=1)
    order = [32 * i + 16 * j + 8 * c for c in range(2) for i in range(4) for j in range(2)]
    hob[...] = jnp.concatenate([head_out[r:r + 8] for r in order], axis=0).astype(jnp.bfloat16)
    loads[7].wait()

    def rc_copy(j):
        begin, width = COLUMNS[j]
        return remote(
            sib_out.at[:, pl.ds(begin, width)], sib_in.at[:, pl.ds(begin, width)], rcs.at[j], rcr.at[j], sibling
        )

    def rx_copies(j):
        begin, width = COLUMNS[j]
        copies = []
        for s in (1, 2, 3):
            to = lax.rem(x + s, 4)
            copies.append(
                remote(
                    x_out.at[pl.ds(pl.multiple_of(16 * to, 16), 16), pl.ds(begin, width)],
                    x_in.at[s - 1, :, pl.ds(begin, width)],
                    rxs.at[j, s - 1],
                    rxr.at[j, s - 1],
                    device(x + s, y, z, core),
                )
            )
        return copies

    def rz_copy(j):
        begin, width = COLUMNS[j][0] // 2, COLUMNS[j][1] // 2
        return remote(
            z_out.at[:, pl.ds(begin, width)], z_in.at[:, pl.ds(begin, width)], rzs.at[j], rzr.at[j],
            device(x, y, z + 8, core),
        )

    theirs = hob[pl.ds(pl.multiple_of(64 * other, 64), 64), :]
    mine = hob[pl.ds(pl.multiple_of(64 * core, 64), 64), :]
    swapped = jnp.concatenate([theirs, mine], axis=0)
    chunks = len(COLUMNS)
    for j in range(chunks + 2):
        if j < chunks:
            columns = slice(COLUMNS[j][0], sum(COLUMNS[j]))
            part = jnp.dot(swapped, wout[:, columns], preferred_element_type=jnp.float32)
            sib_out[:, columns] = part[:64].astype(jnp.bfloat16)
            rc_copy(j).start()
            own[:, columns] = part[64:]
        if j >= 2:
            columns = slice(COLUMNS[j - 2][0], sum(COLUMNS[j - 2]))
            rc_copy(j - 2).wait_recv()
            part = own[:, columns] + sib_in[:, columns].astype(jnp.float32)
            own[:, columns] = part
            x_out[:, columns] = part.astype(jnp.bfloat16)
            for copy in rx_copies(j - 2):
                copy.start()
    pl.semaphore_wait(met, 1)
    for j, (begin, width) in enumerate(COLUMNS):
        columns = slice(begin, begin + width)
        for copy in rx_copies(j):
            copy.wait_recv()
        part = own[pl.ds(pl.multiple_of(16 * x, 16), 16), columns]
        for s in range(3):
            part = part + x_in[s, :, columns].astype(jnp.float32)
        total[:, columns] = part
        away = total[pl.ds(pl.multiple_of(8 - 8 * zhi, 8), 8), columns]
        wide = width // 2
        z_out[:, begin // 2:begin // 2 + wide] = jnp.concatenate([away[:, :wide], away[:, wide:]], axis=0).astype(
            jnp.bfloat16
        )
        rz_copy(j).start()
    for j, (begin, width) in enumerate(COLUMNS):
        columns = slice(begin, begin + width)
        wide = width // 2
        rz_copy(j).wait_recv()
        came = z_in[:, begin // 2:begin // 2 + wide].astype(jnp.float32)
        came = jnp.concatenate([came[:8], came[8:]], axis=1)
        o_ref[:, columns] = (total[pl.ds(pl.multiple_of(8 * zhi, 8), 8), columns] + came).astype(jnp.bfloat16)

    for i in range(7):
        wanted, copy = z_send(i)
        pl.when(wanted)(copy.wait_send)
    for block_z in range(8):
        @pl.when(y == 0)
        def _():
            y_three(block_z).wait_send()
    for g in range(2):
        @pl.when(jnp.logical_not(last_row))
        def _():
            y_group(1, g, y).wait_send()

        @pl.when((y == 1) | last_row)
        def _():
            y_group(2, g, y).wait_send()

    def drain(i, carry):
        @pl.when(needed(i))
        def _():
            x_group(i, 0).wait_send()
            x_group(i, 1).wait_send()
            core_copy(i).wait_send()

        return carry

    lax.fori_loop(0, GROUPS, drain, 0)
    for j in range(len(COLUMNS)):
        rc_copy(j).wait_send()
        for copy in rx_copies(j):
            copy.wait_send()
        rz_copy(j).wait_send()


def body(q_nope, q_rope, latent, rope_keys, seg_ids, w_uk, w_uv, w_out):
    hbm = pl.BlockSpec(memory_space=pl.ANY)
    bf16, f32 = jnp.bfloat16, jnp.float32
    dma, chunks = pltpu.SemaphoreType.DMA, len(COLUMNS)
    return pl.pallas_call(
        kernel,
        out_shape=jax.ShapeDtypeStruct((8, OUT), bf16),
        in_specs=[hbm] * 8,
        out_specs=pl.BlockSpec(memory_space=pltpu.VMEM),
        scratch_shapes=[
            pltpu.VMEM((ROWS, HEADS * NOPE), bf16),
            pltpu.VMEM((ROWS, HEADS * ROPE), bf16),
            pltpu.VMEM((ROWS, LAT), bf16),
            pltpu.VMEM((ROPE, ROWS), bf16),
            pltpu.VMEM((32, 128), jnp.int32),
            pltpu.VMEM((LAT, HEADS * NOPE), bf16),
            pltpu.VMEM((LAT, HEADS * VDIM), bf16),
            pltpu.VMEM((HEADS * VDIM, OUT), bf16),
            pltpu.VMEM((32, 4, TILES, 16, 128), bf16),
            pltpu.VMEM((ROWS, WIDE), bf16),
            pltpu.VMEM((4, TILES, 16, 128), bf16),
            pltpu.VMEM((2, HEADS * ROWS, WIDE), bf16),
            pltpu.VMEM((HEADS * ROWS, LAT), f32),
            pltpu.VMEM((HEADS * ROWS, 128), f32),
            pltpu.VMEM((HEADS * ROWS, 128), f32),
            pltpu.VMEM((ROWS, HEADS * VDIM), bf16),
            pltpu.VMEM((64, OUT), bf16),
            pltpu.VMEM((64, OUT), bf16),
            pltpu.VMEM((64, OUT), f32),
            pltpu.VMEM((64, OUT), bf16),
            pltpu.VMEM((3, 16, OUT), bf16),
            pltpu.VMEM((16, OUT), f32),
            pltpu.VMEM((16, OUT // 2), bf16),
            pltpu.VMEM((16, OUT // 2), bf16),
            pltpu.SemaphoreType.REGULAR,
            dma((8,)),
            dma((7,)), dma((7,)),
            dma((2, 2)), dma((2, 2)),
            dma((8,)), dma((8,)),
            dma((GROUPS, 2)), dma((GROUPS, 2)),
            dma((GROUPS,)), dma((GROUPS,)),
            dma((chunks,)), dma((chunks,)),
            dma((chunks, 3)), dma((chunks, 3)),
            dma((chunks,)), dma((chunks,)),
        ],
        compiler_params=pltpu.CompilerParams(
            collective_id=0, has_side_effects=True, vmem_limit_bytes=VMEM_BYTES
        ),
    )(q_nope, q_rope, latent, rope_keys.T, seg_ids.reshape(32, 128), w_uk, w_uv, w_out)


def solution(mesh):
    placed = (
        P("ctx", "head"),
        P("ctx", "head"),
        P("ctx", None),
        P("ctx", None),
        P(),
        P(None, "head"),
        P(None, "head"),
        P("head", None),
    )
    return jax.shard_map(
        body, mesh=mesh, in_specs=placed, out_specs=P(("ctx", "head"), None), check_vma=False
    )
```

```python
import functools
import math

import jax
import jax.numpy as jnp
from jax import lax
from jax.experimental import pallas as pl
from jax.experimental.pallas import tpu as pltpu
from jax.sharding import PartitionSpec as P

LAT = 512
NOPE = 128
ROPE = 64
VDIM = 128
WIDE = 640
ROWS = 128
HEADS = 4
OUT = 3584
GROUPS = 6
COLUMNS = tuple((512 * i, 512) for i in range(7))
TILES = 9
OWN = 2
VMEM_BYTES = 62 * 2**20
MESH = pl.DeviceIdType.MESH
NT = (((1,), (1,)), ((), ()))


def device(x, y, z, core):
    x, y, z = lax.rem(x, 4), lax.rem(y, 4), lax.rem(z, 16)
    return (y * 8 + lax.rem(z, 8), x * 4 + lax.div(z, 8) * 2 + core)


def remote(src, dst, send, recv, target):
    return pltpu.make_async_remote_copy(
        src_ref=src, dst_ref=dst, send_sem=send, recv_sem=recv, device_id=target, device_id_type=MESH
    )


def kernel(
    qn_hbm, qr_hbm, lat_hbm, rope_hbm, seg_hbm, wuk_hbm, wuv_hbm, wout_hbm, o_ref,
    qn_ref, qr_ref, lat_ref, rope_ref, seg_ref, wuk, wuv, wout,
    kb, keys_ref, kown, qb, acc, m_ref, l_ref, hob, sib_out, sib_in, own, x_out, x_in, total, z_out, z_in,
    met, w_sem, zs, zr, ys, yr, ws, wr, xs, xr, cs, cr, rcs, rcr, rxs, rxr, rzs, rzr,
):
    ctx, head = lax.axis_index("ctx"), lax.axis_index("head")
    y, zlo = lax.div(ctx, 8), lax.rem(ctx, 8)
    x, zhi, core = lax.div(head, 4), lax.rem(lax.div(head, 2), 2), lax.rem(head, 2)
    z = zhi * 8 + zlo
    last_row = y == 3
    other = 1 - core
    sibling = device(x, y, z, other)
    half = 2 * core + lax.rem(x, 2)

    barrier = pltpu.get_barrier_semaphore()
    partners = [device(x, y, z + s, core) for s in (1, 2, 3, 4, 15, 14, 13, 12)]
    partners += [device(x, y + s, z, core) for s in (1, 2, 3)]
    partners += [device(x + s, y, z, core) for s in (1, 2, 3)]
    partners += [sibling]
    for partner in partners:
        pl.semaphore_signal(barrier, inc=1, device_id=partner, device_id_type=MESH)

    pairs = (
        (lat_hbm, lat_ref), (rope_hbm, rope_ref), (wuk_hbm, wuk), (qn_hbm, qn_ref), (qr_hbm, qr_ref),
        (seg_hbm, seg_ref), (wuv_hbm, wuv), (wout_hbm, wout),
    )
    loads = [pltpu.make_async_copy(a, b, w_sem.at[i]) for i, (a, b) in enumerate(pairs)]
    for load in loads:
        load.start()

    loads[0].wait()
    loads[1].wait()
    rope = jnp.transpose(rope_ref[...].astype(jnp.float32)).astype(jnp.bfloat16)
    keys_ref[...] = jnp.concatenate(
        [lat_ref[...], rope, jnp.zeros((ROWS, WIDE - LAT - ROPE), jnp.bfloat16)], axis=1
    )
    for q in range(4):
        for r in range(2):
            at = 32 * q + 16 * r
            for lane in range(4):
                kown[q, 4 * r + lane] = lat_ref[at:at + 16, 128 * lane:128 * lane + 128]
        kown[q, 8] = jnp.concatenate([rope[32 * q:32 * q + 16], rope[32 * q + 16:32 * q + 32]], axis=1)

    @pl.when(jnp.logical_not(last_row))
    def _():
        kb[8 * y + OWN, half] = kown[half]

    pl.semaphore_wait(barrier, len(partners))

    pl.semaphore_signal(met, inc=1, device_id=device(x, y, z + 4, core), device_id_type=MESH)

    steps = [1, 15, 2, 14, 3, 13, 4 + 8 * core]

    slots = [1, 3, 0, 4, 7, 5, 6]

    def block_z(slot):
        return lax.rem(slot + zlo + 8 - OWN, 8)

    def z_send(i):
        wanted = jnp.logical_not(last_row) | (lax.rem(zlo + steps[i], 8) > zlo)
        return wanted, remote(
            kown.at[half], kb.at[8 * y + slots[i], half], zs.at[i], zr.at[i], device(x, y, z + steps[i], core)
        )

    def z_start(i):
        wanted, copy = z_send(i)
        pl.when(wanted)(copy.start)

    def z_recv(i):
        piece = kb.at[8 * y + slots[i], half]
        return remote(piece, piece, zs.at[i], zr.at[i], sibling)

    def y_hop(hop, slot):
        piece = kb.at[y * 8 + slot, half]
        g = slot // 4
        return remote(piece, piece, ys.at[hop - 1, g], yr.at[hop - 1, g], device(x, y + hop, z, core))

    def place_in_last(slot):
        return jnp.where(block_z(slot) >= zlo, 24 + slot, slot)

    def y_three(slot):
        return remote(
            kb.at[slot, half], kb.at[place_in_last(slot), half], ws.at[slot], wr.at[slot], device(x, 3, z, core)
        )

    def y_back(slot):
        g = slot // 4
        return remote(
            kb.at[place_in_last(slot), half], kb.at[slot, half], ys.at[1, g], yr.at[1, g], device(x, 2, z, core)
        )

    def y_group(k, g, row):
        piece = kb.at[pl.ds(row * 8 + 4 * g, 4), half]
        return remote(piece, piece, ys.at[k - 1, g], yr.at[k - 1, g], sibling)

    sides = (jnp.where(core == 0, 1, 3), jnp.where(core == 0, 3, 1))
    parts_of = (pl.ds(0, 4), pl.ds(4, 5))

    def place_of(i):
        return (y - lax.rem(i, 3)) * 8 + 4 * lax.div(i, 3)

    def needed(i):
        k, g = lax.rem(i, 3), lax.div(i, 3)
        return (y >= k) & ((k > 0) | last_row | (zlo >= 1 + 2 * g))

    def x_group(i, side):
        piece = kb.at[pl.ds(place_of(i), 4), half, parts_of[side]]
        return remote(piece, piece, xs.at[i, side], xr.at[i, side], device(x + sides[side], y, z, core))

    def core_copy(i):
        piece = kb.at[pl.ds(place_of(i), 4), pl.ds(2 * core, 2)]
        return remote(piece, piece, cs.at[i], cr.at[i], sibling)

    def forward(slot):
        @pl.when(y == 0)
        def _():
            y_three(slot).start()

        @pl.when(jnp.logical_not(last_row))
        def _():
            y_hop(1, slot).start()

        @pl.when(y == 1)
        def _():
            y_hop(2, slot).start()

    def pass_back(slot):
        @pl.when(last_row)
        def _():
            y_three(slot).wait_recv()
            y_back(slot).start()

    z_start(0)
    z_start(1)
    forward(OWN)

    for load in loads[2:5]:
        load.wait()
    for h in range(HEADS):
        if h:
            if h < 3:
                z_start(2 * h)
                z_start(2 * h + 1)
            else:
                z_start(6)
        absorbed = lax.dot_general(
            qn_ref[:, h * NOPE:(h + 1) * NOPE], wuk[:, h * NOPE:(h + 1) * NOPE], NT, preferred_element_type=jnp.float32
        ).astype(jnp.bfloat16)
        rows = slice(h * ROWS, (h + 1) * ROWS)
        tail = qr_ref[:, h * ROPE:(h + 1) * ROPE]
        for r in range(2):
            qb[r, rows, :LAT] = absorbed
            qb[r, rows, LAT:] = jnp.concatenate([jnp.zeros_like(tail)] * r + [tail] + [jnp.zeros_like(tail)] * (1 - r), axis=1)

    def arrive(i):
        @pl.when(jnp.logical_not(last_row) | (block_z(slots[i]) < zlo))
        def _():
            z_recv(i).wait_recv()

        forward(slots[i])
        pass_back(slots[i])

    def stage_x(i):
        k, g = lax.rem(i, 3), lax.div(i, 3)

        @pl.when((i < GROUPS) & needed(i))
        def _():
            @pl.when(k > 0)
            def _():
                y_group(jnp.maximum(k, 1), g, y - k).wait_recv()

            x_group(i, 0).start()
            x_group(i, 1).start()

    pass_back(OWN)
    for i in range(3):
        arrive(i)
    stage_x(0)

    loads[5].wait()
    seg = seg_ref[...]
    own_seg = seg_ref[pl.ds(ctx, 1), :]
    first = jnp.zeros((1, ROWS), jnp.float32)
    for e in range(7):
        count = jnp.sum(jnp.where(seg == e, 1.0, 0.0), axis=1, keepdims=True)
        count = jnp.sum(count, axis=0, keepdims=True)
        first = first + jnp.where(own_seg > e, count, 0.0)
    down = lax.broadcasted_iota(jnp.int32, (ROWS, ROWS), 0)
    across = lax.broadcasted_iota(jnp.int32, (ROWS, ROWS), 1)
    first = jnp.sum(jnp.where(down == across, first, 0.0), axis=1, keepdims=True).astype(jnp.int32)
    first2 = jnp.concatenate([first] * HEADS, axis=0)
    factor = math.log2(math.e) / math.sqrt(NOPE + ROPE)

    keys = keys_ref[...]
    diagonal = (across <= down) & (across + ctx * ROWS >= first)
    for h in range(HEADS):
        rows = slice(h * ROWS, (h + 1) * ROWS)
        scores = lax.dot_general(qb[0, rows, :], keys, NT, preferred_element_type=jnp.float32) * factor
        scores = jnp.where(diagonal, scores, -jnp.inf)
        top = jnp.broadcast_to(jnp.max(scores, axis=1, keepdims=True), (ROWS, 128))
        powers = jnp.exp2(scores - top)
        m_ref[rows, :] = top
        l_ref[rows, :] = powers
        acc[rows, :] = jnp.dot(powers.astype(jnp.bfloat16), keys[:, :LAT], preferred_element_type=jnp.float32)

    @pl.when(last_row)
    def _():
        stage_x(1)
        stage_x(2)

    for i in range(3, 7):
        arrive(i)

    @pl.when(jnp.logical_not(last_row))
    def _():
        stage_x(1)
        stage_x(2)

    def stage_core(i):
        @pl.when((i < GROUPS) & needed(i))
        def _():
            x_group(i, 0).wait_recv()
            x_group(i, 1).wait_recv()
            core_copy(i).start()

    column = lax.broadcasted_iota(jnp.int32, (1, 512), 1)
    beside = lax.rem(lax.div(column, 64), 4)
    within = (
        lax.rem(lax.div(column, 16), 4) * 32
        + lax.div(column, 256) * 16
        + lax.rem(column, 16)
    )

    def stage_attend(i):
        @pl.when((i >= 0) & needed(jnp.maximum(i, 0)))
        def _():
            core_copy(i).wait_recv()
            begin = place_of(i)
            some = pl.ds(begin, 4)
            lats = [
                jnp.concatenate([kb[some, :, 4 * r + lane].reshape(256, 128) for lane in range(4)], axis=1)
                for r in range(2)
            ]
            ropes = kb[some, :, 8].reshape(256, 128)
            values = jnp.concatenate(lats, axis=0)
            place = (y - lax.rem(i, 3)) * 1024 + block_z(4 * lax.div(i, 3) + beside) * ROWS + within
            place = jnp.where(last_row & (place >= ctx * ROWS), place - 24 * ROWS, place)
            place = jnp.where(place < ctx * ROWS, place, -1)
            visible = place >= first2
            for part in range(1):
                rows = slice(part * 512, (part + 1) * 512)
                scores = jnp.concatenate(
                    [
                        lax.dot_general(
                            qb[r, rows, :], jnp.concatenate([lats[r], ropes], axis=1), NT,
                            preferred_element_type=jnp.float32,
                        )
                        for r in range(2)
                    ],
                    axis=1,
                ) * factor
                scores = jnp.where(visible, scores, -jnp.inf)
                before = m_ref[rows, :]
                top = jnp.maximum(before, jnp.max(scores, axis=1, keepdims=True))
                shrink = jnp.exp2(before - top)
                powers = jnp.exp2(scores - jnp.concatenate([top] * 4, axis=1))
                m_ref[rows, :] = top
                l_ref[rows, :] = l_ref[rows, :] * shrink + (
                    (powers[:, :128] + powers[:, 128:256]) + (powers[:, 256:384] + powers[:, 384:])
                )
                acc[rows, :] = acc[rows, :] * jnp.concatenate([shrink] * 4, axis=1) + jnp.dot(
                    powers.astype(jnp.bfloat16), values, preferred_element_type=jnp.float32
                )

    def step(t, carry):
        stage_core(t)
        stage_x(t + 3)
        stage_attend(t - 1)
        return carry

    lax.fori_loop(0, GROUPS + 1, step, 0)

    loads[6].wait()
    parts = []
    for h in range(HEADS):
        rows = slice(h * ROWS, (h + 1) * ROWS)
        sums = jnp.sum(l_ref[rows, :], axis=1, keepdims=True)
        context = (acc[rows, :] / sums).astype(jnp.bfloat16)
        parts.append(jnp.dot(context, wuv[:, h * VDIM:(h + 1) * VDIM], preferred_element_type=jnp.float32))
    head_out = jnp.concatenate(parts, axis=1)
    order = [32 * i + 16 * j + 8 * c for c in range(2) for i in range(4) for j in range(2)]
    hob[...] = jnp.concatenate([head_out[r:r + 8] for r in order], axis=0).astype(jnp.bfloat16)
    loads[7].wait()

    def rc_copy(j):
        begin, width = COLUMNS[j]
        return remote(
            sib_out.at[:, pl.ds(begin, width)], sib_in.at[:, pl.ds(begin, width)], rcs.at[j], rcr.at[j], sibling
        )

    def rx_copies(j):
        begin, width = COLUMNS[j]
        copies = []
        for s in (1, 2, 3):
            to = lax.rem(x + s, 4)
            copies.append(
                remote(
                    x_out.at[pl.ds(pl.multiple_of(16 * to, 16), 16), pl.ds(begin, width)],
                    x_in.at[s - 1, :, pl.ds(begin, width)],
                    rxs.at[j, s - 1],
                    rxr.at[j, s - 1],
                    device(x + s, y, z, core),
                )
            )
        return copies

    def rz_copy(j):
        begin, width = COLUMNS[j][0] // 2, COLUMNS[j][1] // 2
        return remote(
            z_out.at[:, pl.ds(begin, width)], z_in.at[:, pl.ds(begin, width)], rzs.at[j], rzr.at[j],
            device(x, y, z + 8, core),
        )

    theirs = hob[pl.ds(pl.multiple_of(64 * other, 64), 64), :]
    mine = hob[pl.ds(pl.multiple_of(64 * core, 64), 64), :]
    swapped = jnp.concatenate([theirs, mine], axis=0)
    chunks = len(COLUMNS)
    for j in range(chunks + 2):
        if j < chunks:
            columns = slice(COLUMNS[j][0], sum(COLUMNS[j]))
            part = jnp.dot(swapped, wout[:, columns], preferred_element_type=jnp.float32)
            sib_out[:, columns] = part[:64].astype(jnp.bfloat16)
            rc_copy(j).start()
            own[:, columns] = part[64:]
        if j >= 2:
            columns = slice(COLUMNS[j - 2][0], sum(COLUMNS[j - 2]))
            rc_copy(j - 2).wait_recv()
            part = own[:, columns] + sib_in[:, columns].astype(jnp.float32)
            own[:, columns] = part
            x_out[:, columns] = part.astype(jnp.bfloat16)
            for copy in rx_copies(j - 2):
                copy.start()
    pl.semaphore_wait(met, 1)
    for j, (begin, width) in enumerate(COLUMNS):
        columns = slice(begin, begin + width)
        for copy in rx_copies(j):
            copy.wait_recv()
        part = own[pl.ds(pl.multiple_of(16 * x, 16), 16), columns]
        for s in range(3):
            part = part + x_in[s, :, columns].astype(jnp.float32)
        total[:, columns] = part
        away = total[pl.ds(pl.multiple_of(8 - 8 * zhi, 8), 8), columns]
        wide = width // 2
        z_out[:, begin // 2:begin // 2 + wide] = jnp.concatenate([away[:, :wide], away[:, wide:]], axis=0).astype(
            jnp.bfloat16
        )
        rz_copy(j).start()
    for j, (begin, width) in enumerate(COLUMNS):
        columns = slice(begin, begin + width)
        wide = width // 2
        rz_copy(j).wait_recv()
        came = z_in[:, begin // 2:begin // 2 + wide].astype(jnp.float32)
        came = jnp.concatenate([came[:8], came[8:]], axis=1)
        o_ref[:, columns] = (total[pl.ds(pl.multiple_of(8 * zhi, 8), 8), columns] + came).astype(jnp.bfloat16)

    for i in range(7):
        wanted, copy = z_send(i)
        pl.when(wanted)(copy.wait_send)
    for slot in range(8):
        @pl.when(y == 0)
        def _():
            y_three(slot).wait_send()
    for g in range(2):
        @pl.when(jnp.logical_not(last_row))
        def _():
            y_group(1, g, y).wait_send()

        @pl.when((y == 1) | last_row)
        def _():
            y_group(2, g, y).wait_send()

    def drain(i, carry):
        @pl.when(needed(i))
        def _():
            x_group(i, 0).wait_send()
            x_group(i, 1).wait_send()
            core_copy(i).wait_send()

        return carry

    lax.fori_loop(0, GROUPS, drain, 0)
    for j in range(len(COLUMNS)):
        rc_copy(j).wait_send()
        for copy in rx_copies(j):
            copy.wait_send()
        rz_copy(j).wait_send()


def body(q_nope, q_rope, latent, rope_keys, seg_ids, w_uk, w_uv, w_out):
    hbm = pl.BlockSpec(memory_space=pl.ANY)
    bf16, f32 = jnp.bfloat16, jnp.float32
    dma, chunks = pltpu.SemaphoreType.DMA, len(COLUMNS)
    return pl.pallas_call(
        kernel,
        out_shape=jax.ShapeDtypeStruct((8, OUT), bf16),
        in_specs=[hbm] * 8,
        out_specs=pl.BlockSpec(memory_space=pltpu.VMEM),
        scratch_shapes=[
            pltpu.VMEM((ROWS, HEADS * NOPE), bf16),
            pltpu.VMEM((ROWS, HEADS * ROPE), bf16),
            pltpu.VMEM((ROWS, LAT), bf16),
            pltpu.VMEM((ROPE, ROWS), bf16),
            pltpu.VMEM((32, 128), jnp.int32),
            pltpu.VMEM((LAT, HEADS * NOPE), bf16),
            pltpu.VMEM((LAT, HEADS * VDIM), bf16),
            pltpu.VMEM((HEADS * VDIM, OUT), bf16),
            pltpu.VMEM((32, 4, TILES, 16, 128), bf16),
            pltpu.VMEM((ROWS, WIDE), bf16),
            pltpu.VMEM((4, TILES, 16, 128), bf16),
            pltpu.VMEM((2, HEADS * ROWS, WIDE), bf16),
            pltpu.VMEM((HEADS * ROWS, LAT), f32),
            pltpu.VMEM((HEADS * ROWS, 128), f32),
            pltpu.VMEM((HEADS * ROWS, 128), f32),
            pltpu.VMEM((ROWS, HEADS * VDIM), bf16),
            pltpu.VMEM((64, OUT), bf16),
            pltpu.VMEM((64, OUT), bf16),
            pltpu.VMEM((64, OUT), f32),
            pltpu.VMEM((64, OUT), bf16),
            pltpu.VMEM((3, 16, OUT), bf16),
            pltpu.VMEM((16, OUT), f32),
            pltpu.VMEM((16, OUT // 2), bf16),
            pltpu.VMEM((16, OUT // 2), bf16),
            pltpu.SemaphoreType.REGULAR,
            dma((8,)),
            dma((7,)), dma((7,)),
            dma((2, 2)), dma((2, 2)),
            dma((8,)), dma((8,)),
            dma((GROUPS, 2)), dma((GROUPS, 2)),
            dma((GROUPS,)), dma((GROUPS,)),
            dma((chunks,)), dma((chunks,)),
            dma((chunks, 3)), dma((chunks, 3)),
            dma((chunks,)), dma((chunks,)),
        ],
        compiler_params=pltpu.CompilerParams(
            collective_id=0, has_side_effects=True, vmem_limit_bytes=VMEM_BYTES
        ),
    )(q_nope, q_rope, latent, rope_keys.T, seg_ids.reshape(32, 128), w_uk, w_uv, w_out)


def solution(mesh):
    placed = (
        P("ctx", "head"),
        P("ctx", "head"),
        P("ctx", None),
        P("ctx", None),
        P(),
        P(None, "head"),
        P(None, "head"),
        P("head", None),
    )
    return jax.shard_map(
        body, mesh=mesh, in_specs=placed, out_specs=P(("ctx", "head"), None), check_vma=False
    )
```

```python
import functools
import math

import jax
import jax.numpy as jnp
from jax import lax
from jax.experimental import pallas as pl
from jax.experimental.pallas import tpu as pltpu
from jax.sharding import PartitionSpec as P

LAT = 512
NOPE = 128
ROPE = 64
VDIM = 128
WIDE = 640
ROWS = 128
HEADS = 4
OUT = 3584
GROUPS = 6
COLUMNS = tuple((512 * i, 512) for i in range(7))
TILES = 9
OWN = 2
VMEM_BYTES = 62 * 2**20
MESH = pl.DeviceIdType.MESH
NT = (((1,), (1,)), ((), ()))


def device(x, y, z, core):
    x, y, z = lax.rem(x, 4), lax.rem(y, 4), lax.rem(z, 16)
    return (y * 8 + lax.rem(z, 8), x * 4 + lax.div(z, 8) * 2 + core)


def remote(src, dst, send, recv, target):
    return pltpu.make_async_remote_copy(
        src_ref=src, dst_ref=dst, send_sem=send, recv_sem=recv, device_id=target, device_id_type=MESH
    )


def kernel(
    qn_hbm, qr_hbm, lat_hbm, rope_hbm, seg_hbm, wuk_hbm, wuv_hbm, wout_hbm, o_ref,
    qn_ref, qr_ref, lat_ref, rope_ref, seg_ref, wuk, wuv, wout,
    kb, keys_ref, kown, qb, acc, m_ref, l_ref, hob, sib_out, sib_in, own, x_out, x_in, total, z_out, z_in,
    met, w_sem, zs, zr, ys, yr, ws, wr, xs, xr, cs, cr, rcs, rcr, rxs, rxr, rzs, rzr,
):
    ctx, head = lax.axis_index("ctx"), lax.axis_index("head")
    y, zlo = lax.div(ctx, 8), lax.rem(ctx, 8)
    x, zhi, core = lax.div(head, 4), lax.rem(lax.div(head, 2), 2), lax.rem(head, 2)
    z = zhi * 8 + zlo
    last_row = y == 3
    other = 1 - core
    sibling = device(x, y, z, other)
    half = 2 * core + lax.rem(x, 2)

    barrier = pltpu.get_barrier_semaphore()
    partners = [device(x, y, z + s, core) for s in (1, 2, 3, 4, 15, 14, 13, 12)]
    partners += [device(x, y + s, z, core) for s in (1, 2, 3)]
    partners += [device(x + s, y, z, core) for s in (1, 2, 3)]
    partners += [sibling]
    for partner in partners:
        pl.semaphore_signal(barrier, inc=1, device_id=partner, device_id_type=MESH)

    pairs = (
        (lat_hbm, lat_ref), (rope_hbm, rope_ref), (wuk_hbm, wuk), (qn_hbm, qn_ref), (qr_hbm, qr_ref),
        (seg_hbm, seg_ref), (wuv_hbm, wuv), (wout_hbm, wout),
    )
    loads = [pltpu.make_async_copy(a, b, w_sem.at[i]) for i, (a, b) in enumerate(pairs)]
    for load in loads:
        load.start()

    loads[0].wait()
    loads[1].wait()
    rope = jnp.transpose(rope_ref[...].astype(jnp.float32)).astype(jnp.bfloat16)
    keys_ref[...] = jnp.concatenate(
        [lat_ref[...], rope, jnp.zeros((ROWS, WIDE - LAT - ROPE), jnp.bfloat16)], axis=1
    )
    for q in range(4):
        for r in range(2):
            at = 32 * q + 16 * r
            for lane in range(4):
                kown[q, 4 * r + lane] = lat_ref[at:at + 16, 128 * lane:128 * lane + 128]
        kown[q, 8] = jnp.concatenate([rope[32 * q:32 * q + 16], rope[32 * q + 16:32 * q + 32]], axis=1)

    @pl.when(jnp.logical_not(last_row))
    def _():
        kb[8 * y + OWN, half] = kown[half]

    pl.semaphore_wait(barrier, len(partners))

    pl.semaphore_signal(met, inc=1, device_id=device(x, y, z + 4, core), device_id_type=MESH)

    steps = [1, 15, 2, 14, 3, 13, 4 + 8 * core]

    slots = [1, 3, 0, 4, 7, 5, 6]

    def block_z(slot):
        return lax.rem(slot + zlo + 8 - OWN, 8)

    def z_send(i):
        wanted = jnp.logical_not(last_row) | (lax.rem(zlo + steps[i], 8) > zlo)
        return wanted, remote(
            kown.at[half], kb.at[8 * y + slots[i], half], zs.at[i], zr.at[i], device(x, y, z + steps[i], core)
        )

    def z_start(i):
        wanted, copy = z_send(i)
        pl.when(wanted)(copy.start)

    def z_recv(i):
        piece = kb.at[8 * y + slots[i], half]
        return remote(piece, piece, zs.at[i], zr.at[i], sibling)

    def y_hop(hop, slot):
        piece = kb.at[y * 8 + slot, half]
        g = slot // 4
        return remote(piece, piece, ys.at[hop - 1, g], yr.at[hop - 1, g], device(x, y + hop, z, core))

    def place_in_last(slot):
        return jnp.where(block_z(slot) >= zlo, 24 + slot, slot)

    def y_three(slot):
        return remote(
            kb.at[slot, half], kb.at[place_in_last(slot), half], ws.at[slot], wr.at[slot], device(x, 3, z, core)
        )

    def y_back(slot):
        g = slot // 4
        return remote(
            kb.at[place_in_last(slot), half], kb.at[slot, half], ys.at[1, g], yr.at[1, g], device(x, 2, z, core)
        )

    def y_group(k, g, row):
        piece = kb.at[pl.ds(row * 8 + 4 * g, 4), half]
        return remote(piece, piece, ys.at[k - 1, g], yr.at[k - 1, g], sibling)

    sides = (jnp.where(core == 0, 1, 3), jnp.where(core == 0, 3, 1))
    parts_of = (pl.ds(0, 4), pl.ds(4, 5))

    def place_of(i):
        return (y - lax.rem(i, 3)) * 8 + 4 * lax.div(i, 3)

    def needed(i):
        k, g = lax.rem(i, 3), lax.div(i, 3)
        return (y >= k) & ((k > 0) | last_row | (zlo >= 1 + 2 * g))

    def x_group(i, side):
        piece = kb.at[pl.ds(place_of(i), 4), half, parts_of[side]]
        return remote(piece, piece, xs.at[i, side], xr.at[i, side], device(x + sides[side], y, z, core))

    def core_copy(i, got):
        piece = kb.at[pl.ds(place_of(i), 4), half + got * (1 - 2 * lax.rem(x, 2))]
        return remote(piece, piece, cs.at[i, got], cr.at[i, got], sibling)

    def forward(slot):
        @pl.when(y == 0)
        def _():
            y_three(slot).start()

        @pl.when(jnp.logical_not(last_row))
        def _():
            y_hop(1, slot).start()

        @pl.when(y == 1)
        def _():
            y_hop(2, slot).start()

    def pass_back(slot):
        @pl.when(last_row)
        def _():
            y_three(slot).wait_recv()
            y_back(slot).start()

    z_start(0)
    z_start(1)
    forward(OWN)

    for load in loads[2:5]:
        load.wait()
    for h in range(HEADS):
        if h:
            if h < 3:
                z_start(2 * h)
                z_start(2 * h + 1)
            else:
                z_start(6)
        absorbed = lax.dot_general(
            qn_ref[:, h * NOPE:(h + 1) * NOPE], wuk[:, h * NOPE:(h + 1) * NOPE], NT, preferred_element_type=jnp.float32
        ).astype(jnp.bfloat16)
        rows = slice(h * ROWS, (h + 1) * ROWS)
        tail = qr_ref[:, h * ROPE:(h + 1) * ROPE]
        for r in range(2):
            qb[r, rows, :LAT] = absorbed
            qb[r, rows, LAT:] = jnp.concatenate([jnp.zeros_like(tail)] * r + [tail] + [jnp.zeros_like(tail)] * (1 - r), axis=1)

    def arrive(i):
        @pl.when(jnp.logical_not(last_row) | (block_z(slots[i]) < zlo))
        def _():
            z_recv(i).wait_recv()

        forward(slots[i])
        pass_back(slots[i])

    def stage_x(i):
        k, g = lax.rem(i, 3), lax.div(i, 3)

        @pl.when((i < GROUPS) & needed(i))
        def _():
            @pl.when(k > 0)
            def _():
                y_group(jnp.maximum(k, 1), g, y - k).wait_recv()

            x_group(i, 0).start()
            x_group(i, 1).start()
            core_copy(i, 0).start()

    pass_back(OWN)
    for i in range(3):
        arrive(i)
    stage_x(0)

    loads[5].wait()
    seg = seg_ref[...]
    own_seg = seg_ref[pl.ds(ctx, 1), :]
    first = jnp.zeros((1, ROWS), jnp.float32)
    for e in range(7):
        count = jnp.sum(jnp.where(seg == e, 1.0, 0.0), axis=1, keepdims=True)
        count = jnp.sum(count, axis=0, keepdims=True)
        first = first + jnp.where(own_seg > e, count, 0.0)
    down = lax.broadcasted_iota(jnp.int32, (ROWS, ROWS), 0)
    across = lax.broadcasted_iota(jnp.int32, (ROWS, ROWS), 1)
    first = jnp.sum(jnp.where(down == across, first, 0.0), axis=1, keepdims=True).astype(jnp.int32)
    first2 = jnp.concatenate([first] * HEADS, axis=0)
    factor = math.log2(math.e) / math.sqrt(NOPE + ROPE)

    keys = keys_ref[...]
    diagonal = (across <= down) & (across + ctx * ROWS >= first)
    for h in range(HEADS):
        rows = slice(h * ROWS, (h + 1) * ROWS)
        scores = lax.dot_general(qb[0, rows, :], keys, NT, preferred_element_type=jnp.float32) * factor
        scores = jnp.where(diagonal, scores, -jnp.inf)
        top = jnp.broadcast_to(jnp.max(scores, axis=1, keepdims=True), (ROWS, 128))
        powers = jnp.exp2(scores - top)
        m_ref[rows, :] = top
        l_ref[rows, :] = powers
        acc[rows, :] = jnp.dot(powers.astype(jnp.bfloat16), keys[:, :LAT], preferred_element_type=jnp.float32)

    @pl.when(last_row)
    def _():
        stage_x(1)
        stage_x(2)

    for i in range(3, 7):
        arrive(i)

    @pl.when(jnp.logical_not(last_row))
    def _():
        stage_x(1)
        stage_x(2)

    def stage_core(i):
        @pl.when((i < GROUPS) & needed(i))
        def _():
            x_group(i, 0).wait_recv()
            x_group(i, 1).wait_recv()
            core_copy(i, 1).start()

    column = lax.broadcasted_iota(jnp.int32, (1, 512), 1)
    beside = lax.rem(lax.div(column, 64), 4)
    within = (
        lax.rem(lax.div(column, 16), 4) * 32
        + lax.div(column, 256) * 16
        + lax.rem(column, 16)
    )

    def stage_attend(i):
        @pl.when((i >= 0) & needed(jnp.maximum(i, 0)))
        def _():
            core_copy(i, 0).wait_recv()
            core_copy(i, 1).wait_recv()
            begin = place_of(i)
            some = pl.ds(begin, 4)
            lats = [
                jnp.concatenate([kb[some, :, 4 * r + lane].reshape(256, 128) for lane in range(4)], axis=1)
                for r in range(2)
            ]
            ropes = kb[some, :, 8].reshape(256, 128)
            values = jnp.concatenate(lats, axis=0)
            place = (y - lax.rem(i, 3)) * 1024 + block_z(4 * lax.div(i, 3) + beside) * ROWS + within
            place = jnp.where(last_row & (place >= ctx * ROWS), place - 24 * ROWS, place)
            place = jnp.where(place < ctx * ROWS, place, -1)
            visible = place >= first2
            for part in range(1):
                rows = slice(part * 512, (part + 1) * 512)
                scores = jnp.concatenate(
                    [
                        lax.dot_general(
                            qb[r, rows, :], jnp.concatenate([lats[r], ropes], axis=1), NT,
                            preferred_element_type=jnp.float32,
                        )
                        for r in range(2)
                    ],
                    axis=1,
                ) * factor
                scores = jnp.where(visible, scores, -jnp.inf)
                before = m_ref[rows, :]
                top = jnp.maximum(before, jnp.max(scores, axis=1, keepdims=True))
                shrink = jnp.exp2(before - top)
                powers = jnp.exp2(scores - jnp.concatenate([top] * 4, axis=1))
                m_ref[rows, :] = top
                l_ref[rows, :] = l_ref[rows, :] * shrink + (
                    (powers[:, :128] + powers[:, 128:256]) + (powers[:, 256:384] + powers[:, 384:])
                )
                acc[rows, :] = acc[rows, :] * jnp.concatenate([shrink] * 4, axis=1) + jnp.dot(
                    powers.astype(jnp.bfloat16), values, preferred_element_type=jnp.float32
                )

    plan = (
        (0, stage_x, 3),
        (0, stage_x, 4),
        (0, stage_core, 0),
        (0, stage_core, 1),
        (0, stage_x, 5),
        (0, stage_core, 2),
        (1, stage_core, 3),
        (2, stage_core, 4),
        (3, stage_core, 5),
    )

    def step(t, carry):
        for turn, stage, item in plan:
            @pl.when(t == turn)
            def _():
                stage(item)

        stage_attend(t)
        return carry

    lax.fori_loop(0, GROUPS, step, 0)

    loads[6].wait()
    parts = []
    for h in range(HEADS):
        rows = slice(h * ROWS, (h + 1) * ROWS)
        share = 1.0 / jnp.sum(l_ref[rows, :], axis=1, keepdims=True)
        context = (acc[rows, :] * share).astype(jnp.bfloat16)
        parts.append(jnp.dot(context, wuv[:, h * VDIM:(h + 1) * VDIM], preferred_element_type=jnp.float32))
    head_out = jnp.concatenate(parts, axis=1)
    order = [32 * i + 16 * j + 8 * c for c in range(2) for i in range(4) for j in range(2)]
    hob[...] = jnp.concatenate([head_out[r:r + 8] for r in order], axis=0).astype(jnp.bfloat16)
    loads[7].wait()

    def rc_copy(j):
        begin, width = COLUMNS[j]
        return remote(
            sib_out.at[:, pl.ds(begin, width)], sib_in.at[:, pl.ds(begin, width)], rcs.at[j], rcr.at[j], sibling
        )

    def rx_copies(j):
        begin, width = COLUMNS[j]
        copies = []
        for s in (1, 2, 3):
            to = lax.rem(x + s, 4)
            copies.append(
                remote(
                    x_out.at[pl.ds(pl.multiple_of(16 * to, 16), 16), pl.ds(begin, width)],
                    x_in.at[s - 1, :, pl.ds(begin, width)],
                    rxs.at[j, s - 1],
                    rxr.at[j, s - 1],
                    device(x + s, y, z, core),
                )
            )
        return copies

    def rz_copy(j):
        begin, width = COLUMNS[j][0] // 2, COLUMNS[j][1] // 2
        return remote(
            z_out.at[:, pl.ds(begin, width)], z_in.at[:, pl.ds(begin, width)], rzs.at[j], rzr.at[j],
            device(x, y, z + 8, core),
        )

    theirs = hob[pl.ds(pl.multiple_of(64 * other, 64), 64), :]
    mine = hob[pl.ds(pl.multiple_of(64 * core, 64), 64), :]
    swapped = jnp.concatenate([theirs, mine], axis=0)
    chunks = len(COLUMNS)
    for j in range(chunks + 2):
        if j < chunks:
            columns = slice(COLUMNS[j][0], sum(COLUMNS[j]))
            part = jnp.dot(swapped, wout[:, columns], preferred_element_type=jnp.float32)
            sib_out[:, columns] = part[:64].astype(jnp.bfloat16)
            rc_copy(j).start()
            own[:, columns] = part[64:]
        if j >= 2:
            columns = slice(COLUMNS[j - 2][0], sum(COLUMNS[j - 2]))
            rc_copy(j - 2).wait_recv()
            part = own[:, columns] + sib_in[:, columns].astype(jnp.float32)
            own[:, columns] = part
            x_out[:, columns] = part.astype(jnp.bfloat16)
            for copy in rx_copies(j - 2):
                copy.start()
    pl.semaphore_wait(met, 1)
    for j, (begin, width) in enumerate(COLUMNS):
        columns = slice(begin, begin + width)
        for copy in rx_copies(j):
            copy.wait_recv()
        part = own[pl.ds(pl.multiple_of(16 * x, 16), 16), columns]
        for s in range(3):
            part = part + x_in[s, :, columns].astype(jnp.float32)
        total[:, columns] = part
        away = total[pl.ds(pl.multiple_of(8 - 8 * zhi, 8), 8), columns]
        wide = width // 2
        z_out[:, begin // 2:begin // 2 + wide] = jnp.concatenate([away[:, :wide], away[:, wide:]], axis=0).astype(
            jnp.bfloat16
        )
        rz_copy(j).start()
    for i in range(7):
        wanted, copy = z_send(i)
        pl.when(wanted)(copy.wait_send)
    for slot in range(8):
        @pl.when(y == 0)
        def _():
            y_three(slot).wait_send()
    for g in range(2):
        @pl.when(jnp.logical_not(last_row))
        def _():
            y_group(1, g, y).wait_send()

        @pl.when((y == 1) | last_row)
        def _():
            y_group(2, g, y).wait_send()

    def drain(i, carry):
        @pl.when(needed(i))
        def _():
            x_group(i, 0).wait_send()
            x_group(i, 1).wait_send()
            core_copy(i, 0).wait_send()
            core_copy(i, 1).wait_send()

        return carry

    lax.fori_loop(0, GROUPS, drain, 0)
    for j in range(len(COLUMNS)):
        rc_copy(j).wait_send()
        for copy in rx_copies(j):
            copy.wait_send()

    for j, (begin, width) in enumerate(COLUMNS):
        columns = slice(begin, begin + width)
        wide = width // 2
        rz_copy(j).wait_recv()
        came = z_in[:, begin // 2:begin // 2 + wide].astype(jnp.float32)
        came = jnp.concatenate([came[:8], came[8:]], axis=1)
        o_ref[:, columns] = (total[pl.ds(pl.multiple_of(8 * zhi, 8), 8), columns] + came).astype(jnp.bfloat16)

    for j in range(len(COLUMNS)):
        rz_copy(j).wait_send()


def body(q_nope, q_rope, latent, rope_keys, seg_ids, w_uk, w_uv, w_out):
    hbm = pl.BlockSpec(memory_space=pl.ANY)
    bf16, f32 = jnp.bfloat16, jnp.float32
    dma, chunks = pltpu.SemaphoreType.DMA, len(COLUMNS)
    return pl.pallas_call(
        kernel,
        out_shape=jax.ShapeDtypeStruct((8, OUT), bf16),
        in_specs=[hbm] * 8,
        out_specs=pl.BlockSpec(memory_space=pltpu.VMEM),
        scratch_shapes=[
            pltpu.VMEM((ROWS, HEADS * NOPE), bf16),
            pltpu.VMEM((ROWS, HEADS * ROPE), bf16),
            pltpu.VMEM((ROWS, LAT), bf16),
            pltpu.VMEM((ROPE, ROWS), bf16),
            pltpu.VMEM((32, 128), jnp.int32),
            pltpu.VMEM((LAT, HEADS * NOPE), bf16),
            pltpu.VMEM((LAT, HEADS * VDIM), bf16),
            pltpu.VMEM((HEADS * VDIM, OUT), bf16),
            pltpu.VMEM((32, 4, TILES, 16, 128), bf16),
            pltpu.VMEM((ROWS, WIDE), bf16),
            pltpu.VMEM((4, TILES, 16, 128), bf16),
            pltpu.VMEM((2, HEADS * ROWS, WIDE), bf16),
            pltpu.VMEM((HEADS * ROWS, LAT), f32),
            pltpu.VMEM((HEADS * ROWS, 128), f32),
            pltpu.VMEM((HEADS * ROWS, 128), f32),
            pltpu.VMEM((ROWS, HEADS * VDIM), bf16),
            pltpu.VMEM((64, OUT), bf16),
            pltpu.VMEM((64, OUT), bf16),
            pltpu.VMEM((64, OUT), f32),
            pltpu.VMEM((64, OUT), bf16),
            pltpu.VMEM((3, 16, OUT), bf16),
            pltpu.VMEM((16, OUT), f32),
            pltpu.VMEM((16, OUT // 2), bf16),
            pltpu.VMEM((16, OUT // 2), bf16),
            pltpu.SemaphoreType.REGULAR,
            dma((8,)),
            dma((7,)), dma((7,)),
            dma((2, 2)), dma((2, 2)),
            dma((8,)), dma((8,)),
            dma((GROUPS, 2)), dma((GROUPS, 2)),
            dma((GROUPS, 2)), dma((GROUPS, 2)),
            dma((chunks,)), dma((chunks,)),
            dma((chunks, 3)), dma((chunks, 3)),
            dma((chunks,)), dma((chunks,)),
        ],
        compiler_params=pltpu.CompilerParams(
            collective_id=0, has_side_effects=True, vmem_limit_bytes=VMEM_BYTES
        ),
    )(q_nope, q_rope, latent, rope_keys.T, seg_ids.reshape(32, 128), w_uk, w_uv, w_out)


def solution(mesh):
    placed = (
        P("ctx", "head"),
        P("ctx", "head"),
        P("ctx", None),
        P("ctx", None),
        P(),
        P(None, "head"),
        P(None, "head"),
        P("head", None),
    )
    return jax.shard_map(
        body, mesh=mesh, in_specs=placed, out_specs=P(("ctx", "head"), None), check_vma=False
    )
```
